128 devices in a mesh: pp: 8 (over x, z_hi), ep: 16 (over y, z_lo, core).
Axes of the slice: x: 4, y: 4, z: 4 (z_hi: 2, z_lo: 2; z = z_hi * 2 + z_lo), core: 2. Of those that a mesh axis runs over, the one named last changes fastest.
Arguments:
- state_a: bfloat16 [8, 2048, 7168], P('pp', 'ep'), may hold values from -6 to 6
- state_b: bfloat16 [8, 2048, 7168], P('pp', 'ep'), may hold values from -6 to 6
- enter_a: bfloat16 [2048, 7168], P('ep'), may hold values from -6 to 6
- enter_b: bfloat16 [2048, 7168], P('ep'), may hold values from -6 to 6
- route_a: int32 [8, 2048, 1], P('pp', 'ep'), may hold values from 0 to 3; in each aligned block of 128 rows (0 to 127, 128 to 255, ..., all dimensions but the last counted through in order) at most 40 rows name the same one
- route_b: int32 [8, 2048, 1], P('pp', 'ep'), may hold values from 0 to 3; in each aligned block of 128 rows (0 to 127, 128 to 255, ..., all dimensions but the last counted through in order) at most 40 rows name the same one
- weight_a: float32 [8, 2048, 1], P('pp', 'ep'), may hold values from 0.5 to 2
- weight_b: float32 [8, 2048, 1], P('pp', 'ep'), may hold values from 0.5 to 2
- norm_gain: float32 [8, 7168], P('pp'), may hold values from 0.1 to 1.9
- w_gate: bfloat16 [8, 4096, 7168], P('pp', 'ep'), may hold values from -0.0625 to 0.0625
- w_up: bfloat16 [8, 4096, 7168], P('pp', 'ep'), may hold values from -0.0625 to 0.0625
- w_down: bfloat16 [8, 4096, 7168], P('pp', 'ep'), may hold values from -0.1875 to 0.1875
Outputs:
- new_a: bfloat16 [8, 2048, 7168], P('pp', 'ep')
- new_b: bfloat16 [8, 2048, 7168], P('pp', 'ep')
The draws below stay inside these ranges and needn't reach their ends.
Inputs may be any that keep to these rules, and one draw needn't show every extreme that they name: `route_a`: among the routes of one device's 128 tokens at one section, no expert is named more than 40 times, a bound that some block reaches; every expert is named somewhere. `route_b`: as for route_a.
All inputs are finite; a program needn't handle non-finite values.
Results may differ from the reference program's by a relative error of at most 0.0054.
Values may be sent and summed in bfloat16 or wider, within the bound.
A program may use at most 256 MiB of HBM per device.

```python
import math
import jax
import jax.numpy as jnp
import numpy as np
from jax import lax

D = 7168
FF = 1024
EGROUP = 4
TOPK = 1
TOK_DEV = 128
EXPERTS = 4
CAP = 40
TOKENS = 2048
N_PP = 8
N_EP = 16


def level_of(rng, extent, cuts, least, largest):
    factor_of, own = 1.0, jax.random.fold_in(rng, 6)
    for dim, parts in cuts:
        draws = jnp.exp(jax.random.uniform(jax.random.fold_in(own, dim), (parts,), jnp.float32, least / len(cuts), largest / len(cuts)))
        factor_of = factor_of * jnp.repeat(draws, extent[dim] // parts).reshape([-1 if axis == dim else 1 for axis in range(len(extent))])
    return factor_of


def deal_out(stream_key, own, number, rows, count, top, bound, lean):
    order = jax.random.permutation(stream_key, count)
    crowded, common = portions_of(count, rows * top, bound, lean, True), portions_of(count, rows * top, bound, lean, False)
    places = jnp.arange(count)

    def named(tallies, rotation):
        used = int((tallies > 0).sum())
        fixed = max(1, used // 4)
        moved = fixed + (places - fixed + rotation * (used - fixed)) % max(1, count - fixed)
        return jnp.zeros((count,), jnp.int32).at[order[jnp.where(places < fixed, places, moved)]].set(jnp.asarray(tallies, jnp.int32))

    tallies = jnp.where(number % 4 == 0, named(crowded, number // 4), named(common, number - number // 4 - 1))
    mixed = jax.random.permutation(jax.random.fold_in(own, 3), count)
    donor, taker = mixed[0:count // 2 * 2:2], mixed[1:count // 2 * 2:2]
    slack = jnp.minimum(tallies[donor] - 1, bound - tallies[taker]) // 2
    slack = jnp.where((donor == order[0]) | (taker == order[0]) | (tallies[taker] == 0), 0, jnp.maximum(slack, 0))
    moved = jax.random.randint(jax.random.fold_in(own, 4), (count // 2,), 0, 1 << 20) % (slack + 1)
    tallies = tallies.at[donor].add(-moved).at[taker].add(moved)
    labels = jnp.searchsorted(jnp.cumsum(tallies), jnp.arange(rows * top), side="right").astype(jnp.int32)
    table = labels.reshape(top, rows).T
    table = table[jax.random.permutation(jax.random.fold_in(own, 1), rows)]
    rotation = jax.random.randint(jax.random.fold_in(own, 2), (rows, 1), 0, top)
    return jnp.take_along_axis(table, (jnp.arange(top)[None, :] + rotation) % top, axis=1)


def portions_of(amount, total, limit, skew, full):
    loads = [(1 << 20) // math.isqrt(rank ** skew) + 1 for rank in range(1, amount + 1)]
    largest = limit if full else min(limit, max(-(-total // amount), total * loads[0] // sum(loads)))
    least = 1 if total - largest >= amount - 1 else 0
    counts, rest = [largest] + [least] * (amount - 1), total - largest - least * (amount - 1)
    while rest > 0:
        candidates = [i for i in range(1, amount) if counts[i] < largest] or [i for i in range(1, amount) if counts[i] < limit]
        mass, budget = sum([loads[i] for i in candidates]), rest
        for i in candidates:
            extra = min(limit - counts[i], max(1, budget * loads[i] // mass), rest)
            counts[i] = counts[i] + extra
            rest = rest - extra
    return np.array(counts)


def bell_draw(stream_key, dims, deviation, most, pieces=(), kind=jnp.bfloat16):
    level = level_of(stream_key, dims, pieces, -0.22, 0.18) if pieces else 1.0
    drawn = jax.random.normal(stream_key, dims, jnp.float32) * deviation * level
    return jnp.minimum(jnp.maximum(drawn, -most), most).astype(kind)


def setup_inputs(seed: int = 0) -> dict:
    key_list = jax.random.split(jax.random.key(seed), 13)
    state_a = bell_draw(key_list[0], (N_PP, TOKENS, D), 1.0, 6.0, ((0, 8), (1, 16)))
    state_b = bell_draw(key_list[1], (N_PP, TOKENS, D), 1.0, 6.0, ((0, 8), (1, 16)))
    enter_a = bell_draw(key_list[2], (TOKENS, D), 1.0, 6.0, ((0, 16),))
    enter_b = bell_draw(key_list[3], (TOKENS, D), 1.0, 6.0, ((0, 16),))
    route_a_keys = jax.random.split(jax.random.fold_in(key_list[4], 1), N_PP * TOKENS // TOK_DEV)
    route_a_turns = jax.random.permutation(jax.random.fold_in(key_list[4], 3), N_PP * TOKENS // TOK_DEV)
    route_a = jax.vmap(lambda own, number: deal_out(jax.random.fold_in(key_list[4], 2), own, number, TOK_DEV, EXPERTS, TOPK, CAP, 2))(route_a_keys, route_a_turns).reshape((N_PP, TOKENS, TOPK))
    route_b_keys = jax.random.split(jax.random.fold_in(key_list[5], 1), N_PP * TOKENS // TOK_DEV)
    route_b_turns = jax.random.permutation(jax.random.fold_in(key_list[5], 3), N_PP * TOKENS // TOK_DEV)
    route_b = jax.vmap(lambda own, number: deal_out(jax.random.fold_in(key_list[5], 2), own, number, TOK_DEV, EXPERTS, TOPK, CAP, 2))(route_b_keys, route_b_turns).reshape((N_PP, TOKENS, TOPK))
    weight_a = jnp.clip(jnp.exp(math.log(2.0) - 1.3862944 * jax.random.uniform(key_list[6], (N_PP, TOKENS, TOPK), jnp.float32) ** level_of(key_list[6], (N_PP, TOKENS, TOPK), ((0, 8), (1, 16)), -0.2, 0.2)), 0.5, 2.0)
    weight_b = jnp.clip(jnp.exp(math.log(2.0) - 1.3862944 * jax.random.uniform(key_list[7], (N_PP, TOKENS, TOPK), jnp.float32) ** level_of(key_list[7], (N_PP, TOKENS, TOPK), ((0, 8), (1, 16)), -0.2, 0.2)), 0.5, 2.0)
    norm_gain = jnp.clip(1.0 + 0.18 * jax.random.normal(key_list[8], (N_PP, D), jnp.float32), 0.1, 1.9)
    w_gate = bell_draw(key_list[9], (N_PP, EXPERTS * FF, D), D ** -0.5, 0.0625, ((0, 8), (1, 16)))
    w_up = bell_draw(key_list[10], (N_PP, EXPERTS * FF, D), D ** -0.5, 0.0625, ((0, 8), (1, 16)))
    w_down = bell_draw(key_list[11], (N_PP, EXPERTS * FF, D), FF ** -0.5, 0.1875, ((0, 8), (1, 16)))
    return dict(state_a=state_a, state_b=state_b, enter_a=enter_a, enter_b=enter_b, route_a=route_a, route_b=route_b, weight_a=weight_a, weight_b=weight_b, norm_gain=norm_gain, w_gate=w_gate, w_up=w_up, w_down=w_down)


def normalize(state, gain):
    widened = state.astype(jnp.float32)
    inverse = lax.rsqrt(lax.optimization_barrier(jnp.mean(widened * widened, axis=-1, keepdims=True)) + 1e-06)
    return (widened * inverse * gain).astype(jnp.bfloat16)

def slot_targets(routes):
    onehot = (routes[..., None] == jnp.arange(EXPERTS, dtype=jnp.int32)).astype(jnp.int32)
    earlier = jnp.cumsum(onehot, axis=1) - onehot
    slot_ids = lax.optimization_barrier(jnp.sum(earlier * onehot, axis=-1)).astype(jnp.int32)
    return (routes * CAP + slot_ids).astype(jnp.int32)

def layer(state, routes, weights, gain, w_gate, w_up, w_down):
    normed = normalize(state, gain)
    target = slot_targets(routes.reshape(N_EP, TOK_DEV * TOPK))
    repeated = jnp.repeat(normed.reshape(N_EP, TOK_DEV, D), TOPK, axis=1)
    source_ids = jnp.arange(N_EP, dtype=jnp.int32)[:, None]
    buffer = jnp.zeros((N_EP, EXPERTS * CAP, D), jnp.bfloat16).at[source_ids, target].set(repeated)
    share = FF // EGROUP
    outputs = []
    for expert_id in range(EXPERTS):
        token_rows = buffer[:, expert_id * CAP:(expert_id + 1) * CAP].reshape(N_EP * CAP, D)
        total = jnp.zeros((N_EP * CAP, D), jnp.float32)
        for part_id in range(EGROUP):
            first_row = expert_id * FF + part_id * share
            gate_proj = jnp.dot(token_rows, w_gate[first_row:first_row + share].T, preferred_element_type=jnp.float32)
            up_proj = jnp.dot(token_rows, w_up[first_row:first_row + share].T, preferred_element_type=jnp.float32)
            hidden = (jax.nn.silu(gate_proj) * up_proj).astype(jnp.bfloat16)
            partial_value = jnp.dot(hidden, w_down[first_row:first_row + share], preferred_element_type=jnp.float32).astype(jnp.bfloat16)
            total = total + partial_value.astype(jnp.float32)
        outputs.append(total.reshape(N_EP, CAP, D))
    combined = jnp.concatenate(outputs, axis=1)
    taken = jnp.take_along_axis(combined, target[..., None], axis=1)
    branch = lax.optimization_barrier(jnp.sum(taken.reshape(N_EP, TOK_DEV, TOPK, D) * weights.reshape(N_EP, TOK_DEV, TOPK, 1), axis=2))
    return (state.astype(jnp.float32) + branch.reshape(TOKENS, D)).astype(jnp.bfloat16)

def reference(state_a, state_b, enter_a, enter_b, route_a, route_b, weight_a, weight_b, norm_gain, w_gate, w_up, w_down):
    results_a = []
    results_b = []
    for section_id in range(N_PP):
        incoming_a = enter_a if section_id == 0 else state_a[section_id - 1]
        incoming_b = enter_b if section_id == N_PP - 1 else state_b[section_id + 1]
        results_a.append(layer(incoming_a, route_a[section_id], weight_a[section_id], norm_gain[section_id], w_gate[section_id], w_up[section_id], w_down[section_id]))
        results_b.append(layer(incoming_b, route_b[section_id], weight_b[section_id], norm_gain[section_id], w_gate[section_id], w_up[section_id], w_down[section_id]))
    return (jnp.stack(results_a), jnp.stack(results_b))
```

```python
import functools

import jax
import jax.numpy as jnp
from jax import lax
from jax.experimental import pallas as pl
from jax.experimental.pallas import tpu as pltpu
from jax.sharding import PartitionSpec as P

EGROUP = 4
MESH = pl.DeviceIdType.MESH
BF16 = jnp.bfloat16
F32 = jnp.float32

HOPS = 8
SEND_COLS = 1024
OUT_COLS = 512


def iota(shape, dim):
    return lax.broadcasted_iota(jnp.int32, shape, dim)


def copy_wait(ref, sem):
    pltpu.make_async_copy(ref, ref, sem).wait()


def relay_kernel(
    sections,
    route_ref,
    gain_ref,
    state_a,
    state_b,
    enter_a,
    enter_b,
    w_gate,
    w_up,
    w_down,
    home_a,
    home_b,
    returned,
    xbuf,
    tgt_own,
    tgt_far,
    inv_ref,
    sel_ref,
    sendbuf,
    rows_ref,
    wgu,
    wd,
    acc,
    hs,
    hid,
    local_sem,
    tgt_sems,
    hi_send,
    arr_sem,
    home_sem,
    lo_send,
    out_sem,
    disp_send,
    disp_recv,
    disp_local,
    core_send,
    core_recv,
    hid_send,
    hid_recv,
    wd_send,
    wd_recv,
    ret_send,
    ret_recv,
):
    tok, width = state_a.shape
    share = w_gate.shape[0]
    half = width // 2
    cap2 = sendbuf.shape[2]
    cap = cap2 // 2
    chunk = tok // HOPS
    send_steps = width // SEND_COLS
    out_steps = half // OUT_COLS
    states, enters, homes = (state_a, state_b), (enter_a, enter_b), (home_a, home_b)

    p = lax.axis_index("pp")
    ep = lax.axis_index("ep")
    y, z, c = ep // 4, (ep // 2) % 2, ep % 2
    last = sections - 1

    def at(yy, zz, cc):
        return (p, yy * 4 + zz * 2 + cc)

    def turn(d):
        return (y + d) % 4

    far = y * 4 + (1 - z) * 2 + c
    first = (p == 0, p == last)
    ahead = (p + 1, p - 1)
    goes = (p < last, p > 0)

    load_gate = pltpu.make_async_copy(w_gate, wgu.at[pl.ds(0, share)], local_sem.at[0])
    load_up = pltpu.make_async_copy(w_up, wgu.at[pl.ds(share, share)], local_sem.at[1])
    part = z * 2 + c
    own_cols = pl.ds(pl.multiple_of(c * half, 128), half)
    load_down = pltpu.make_async_copy(w_down.at[:, own_cols], wd.at[part], local_sem.at[2])
    load_gate.start()
    load_up.start()
    load_down.start()

    barrier = pltpu.get_barrier_semaphore()

    def greet(device):
        pl.semaphore_signal(barrier, inc=1, device_id=device, device_id_type=MESH)

    for d in range(4):
        for cc in range(2):
            if d or cc:
                greet(at(turn(d), z, (c + cc) % 2))
    greet(at(y, 1 - z, c))
    greet(at(y, 1 - z, 1 - c))
    for s in range(2):

        @pl.when(goes[s])
        def _():
            greet((ahead[s], far))

    pl.semaphore_wait(barrier, 9 + (p + last - 1) // last + (2 * last - 1 - p) // last)

    def rows_of(i):
        return pl.ds(pl.multiple_of(i * chunk, chunk), chunk)

    def hop(s, i):
        return pltpu.make_async_remote_copy(
            states[s].at[rows_of(i)],
            xbuf.at[s, 1, rows_of(i)],
            hi_send.at[s],
            arr_sem.at[s, i],
            device_id=(ahead[s], far),
            device_id_type=MESH,
        )

    def enter_across(s, i):
        return pltpu.make_async_remote_copy(
            enters[s].at[rows_of(i)],
            xbuf.at[s, 1, rows_of(i)],
            lo_send.at[s],
            arr_sem.at[s, i],
            device_id=(p, far),
            device_id_type=MESH,
        )

    def enter_here(s, i):
        return pltpu.make_async_copy(
            enters[s].at[rows_of(i)], xbuf.at[s, 0, rows_of(i)], home_sem.at[s, i]
        )

    def across(s, i):
        return pltpu.make_async_remote_copy(
            xbuf.at[s, 1, rows_of(i)],
            xbuf.at[s, 0, rows_of(i)],
            lo_send.at[s],
            home_sem.at[s, i],
            device_id=(p, far),
            device_id_type=MESH,
        )

    def begin(s):
        @pl.when(goes[s])
        def _():
            @pl.loop(0, HOPS)
            def _(i):
                hop(s, i).start()

        @pl.when(first[s])
        def _():
            @pl.loop(0, HOPS)
            def _(i):
                enter_across(s, i).start()
                enter_here(s, i).start()

    def wd_copy(k, n):
        zz, cc = (z, 1 - c) if k == 0 else (1 - z, c if k == 1 else 1 - c)
        cols = pl.ds(pl.multiple_of(cc * half + n * OUT_COLS, 128), OUT_COLS)
        return pltpu.make_async_remote_copy(
            w_down.at[:, cols],
            wd.at[part, :, pl.ds(pl.multiple_of(n * OUT_COLS, 128), OUT_COLS)],
            wd_send.at[k],
            wd_recv.at[k, n],
            device_id=at(y, zz, cc),
            device_id_type=MESH,
        )

    def wd_wait(k, n):
        zz, cc = (z, 1 - c) if k == 0 else (1 - z, c if k == 1 else 1 - c)
        copy_wait(
            wd.at[zz * 2 + cc, :, pl.ds(pl.multiple_of(n * OUT_COLS, 128), OUT_COLS)],
            wd_recv.at[k, n],
        )

    begin(0)

    tri = (iota((tok, tok), 0) < iota((tok, tok), 1)).astype(BF16)
    slot_rows = []
    for s in range(2):
        route = route_ref[s : s + 1, :]
        onehot = (iota((16, tok), 0) == route).astype(F32)
        earlier = jnp.dot(onehot.astype(BF16), tri, preferred_element_type=F32)
        rank = jnp.sum(onehot * earlier, axis=0, keepdims=True)
        slot_rows.append(route.astype(F32) * cap + rank)
    tgt_own[...] = jnp.concatenate(slot_rows + [jnp.zeros((6, tok), F32)], axis=0)
    tgt_copy = pltpu.make_async_remote_copy(
        tgt_own,
        tgt_far,
        tgt_sems.at[0],
        tgt_sems.at[1],
        device_id=(p, far),
        device_id_type=MESH,
    )
    tgt_copy.start()

    def stats(s, rel, i):
        block = xbuf[s, rel, rows_of(i), :].astype(F32)
        mean = jnp.mean(block * block, axis=-1, keepdims=True)
        inv_ref[pl.ds(pl.multiple_of(rel * tok + i * chunk, chunk), chunk), :] = jnp.broadcast_to(
            lax.rsqrt(mean + 1e-06), (chunk, 128)
        )

    def arrive(s):
        @pl.loop(0, HOPS)
        def _(i):
            copy_wait(xbuf.at[s, 1, rows_of(i)], arr_sem.at[s, i])

            @pl.when(jnp.logical_not(first[s]))
            def _():
                across(s, i).start()

            if s == 0:

                @pl.when(i == HOPS - 2)
                def _():
                    begin(1)

            if s == 1:

                @pl.when(i == HOPS - 1)
                def _():
                    @pl.loop(0, out_steps)
                    def _(n):
                        for k in range(3):
                            wd_copy(k, n).start()

            stats(s, 1, i)

            @pl.when(i > 0)
            def _():
                copy_wait(xbuf.at[s, 0, rows_of(i - 1)], home_sem.at[s, i - 1])
                stats(s, 0, i - 1)

        copy_wait(xbuf.at[s, 0, rows_of(HOPS - 1)], home_sem.at[s, HOPS - 1])
        stats(s, 0, HOPS - 1)
        pltpu.make_async_copy(xbuf.at[s, 0], homes[s], out_sem.at[s]).start()

    def send_cols(j):
        return pl.ds(pl.multiple_of(j * SEND_COLS, 128), SEND_COLS)

    def disp(s, d, j):
        e = turn(d)
        return pltpu.make_async_remote_copy(
            sendbuf.at[s, e, :, send_cols(j)],
            rows_ref.at[s, c * 4 + y, :, send_cols(j)],
            disp_send.at[s, d - 1],
            disp_recv.at[s, d - 1, j],
            device_id=at(e, z, c),
            device_id_type=MESH,
        )

    def disp_here(s, j):
        return pltpu.make_async_copy(
            sendbuf.at[s, y, :, send_cols(j)],
            rows_ref.at[s, c * 4 + y, :, send_cols(j)],
            disp_local.at[s, j],
        )

    def dispatch(s):
        r = iota((4 * cap2, tok), 0)
        expert = sum((r >= cap2 * k).astype(jnp.int32) for k in range(1, 4))
        rem = r - expert * cap2
        rel = (rem >= cap).astype(jnp.int32)
        value = (expert * cap + rem - rel * cap).astype(F32)
        here = jnp.where((value == tgt_own[s : s + 1, :]) & (rel == 0), 1.0, 0.0)
        there = jnp.where((value == tgt_far[s : s + 1, :]) & (rel == 1), 1.0, 0.0)
        sel_ref[...] = jnp.concatenate([here, there], axis=1).astype(BF16)

        @pl.loop(0, send_steps)
        def _(j):
            for part_no in range(SEND_COLS // 512):
                cols = pl.ds(pl.multiple_of(j * SEND_COLS + part_no * 512, 128), 512)
                x = xbuf[s, :, :, cols].reshape(2 * tok, 512).astype(F32)
                normed = (x * inv_ref[:, 0:1] * gain_ref[:, cols]).astype(BF16)
                picked = jnp.dot(sel_ref[...], normed, preferred_element_type=F32)
                sendbuf[s, :, :, cols] = picked.astype(BF16).reshape(4, cap2, 512)
            for d in (1, 3, 2):
                disp(s, d, j).start()
            disp_here(s, j).start()

    def cores(s, j):
        block = rows_ref.at[s, pl.ds(c * 4, 4), :, send_cols(j)]
        return pltpu.make_async_remote_copy(
            block,
            block,
            core_send.at[s],
            core_recv.at[s, j],
            device_id=at(y, z, 1 - c),
            device_id_type=MESH,
        )

    def project(s, j):
        copy_wait(
            rows_ref.at[s, pl.ds((1 - c) * 4, 4), :, send_cols(j)], core_recv.at[s, j]
        )
        lhs = rows_ref[s, :, :, send_cols(j)].reshape(8 * cap2, SEND_COLS)
        acc[...] += lax.dot_general(
            lhs, wgu[:, send_cols(j)], (((1,), (1,)), ((), ())), preferred_element_type=F32
        )

    def hid_copy(s, k):
        zz, cc = (z, 1 - c) if k == 0 else (1 - z, c if k == 1 else 1 - c)
        return pltpu.make_async_remote_copy(
            hs.at[s, 0 if k == 0 else 1],
            hid.at[s, part],
            hid_send.at[s, k],
            hid_recv.at[s, k],
            device_id=at(y, zz, cc),
            device_id_type=MESH,
        )

    def hid_wait(s, k):
        zz, cc = (z, 1 - c) if k == 0 else (1 - z, c if k == 1 else 1 - c)
        copy_wait(hid.at[s, zz * 2 + cc], hid_recv.at[s, k])

    def hidden(s):
        acc[...] = jnp.zeros_like(acc)

        @pl.loop(0, send_steps)
        def _(j):
            for d in (1, 3, 2):
                copy_wait(
                    rows_ref.at[s, c * 4 + turn(4 - d), :, send_cols(j)],
                    disp_recv.at[s, d - 1, j],
                )
            disp_here(s, j).wait()
            cores(s, j).start()

            @pl.when(j > 0)
            def _():
                project(s, j - 1)

        project(s, send_steps - 1)
        gate, up = acc[:, :share], acc[:, share:]
        h = gate / (1.0 + jnp.exp(-gate)) * up
        mine = [h[b * cap2 : b * cap2 + cap] for b in range(8)]
        others = [h[b * cap2 + cap : (b + 1) * cap2] for b in range(8)]
        hs[s, 0] = jnp.concatenate(mine, axis=0).astype(BF16)
        hs[s, 1] = jnp.concatenate(others, axis=0).astype(BF16)
        for k in (1, 2, 0):
            hid_copy(s, k).start()
        hid[s, part] = hs[s, 0]

    def back(k, n):
        d, cc = k // 2, k % 2
        yy = turn(d)
        to = (c + cc) % 2
        src = sendbuf.at[0, yy, :, pl.ds(pl.multiple_of(to * half + n * OUT_COLS, 128), OUT_COLS)]
        dst = returned.at[y, :, pl.ds(pl.multiple_of(c * half + n * OUT_COLS, 128), OUT_COLS)]
        if k == 0:
            return pltpu.make_async_copy(src, dst, ret_recv.at[0])
        return pltpu.make_async_remote_copy(
            src, dst, ret_send.at[k], ret_recv.at[k], device_id=at(yy, z, to), device_id_type=MESH
        )

    def down(n):
        for k in range(3):
            wd_wait(k, n)
        cols = pl.ds(pl.multiple_of(n * OUT_COLS, 128), OUT_COLS)
        outs = []
        for s in range(2):
            out = jnp.zeros((8 * cap, OUT_COLS), F32)
            for g in range(EGROUP):
                out += jnp.dot(hid[s, g], wd[g, :, cols], preferred_element_type=F32)
            outs.append(out)
        for cc in range(2):
            rows = []
            for b in range(4 * cc, 4 * cc + 4):
                rows += [out[b * cap : (b + 1) * cap] for out in outs]
            to = pl.ds(pl.multiple_of(cc * half + n * OUT_COLS, 128), OUT_COLS)
            sendbuf[0, :, :, to] = (
                jnp.concatenate(rows, axis=0).astype(BF16).reshape(4, cap2, OUT_COLS)
            )
        for k in (2, 3, 6, 7, 4, 5, 1, 0):
            back(k, n).start()

    arrive(0)
    tgt_copy.wait()
    dispatch(0)
    arrive(1)
    dispatch(1)
    load_gate.wait()
    load_up.wait()
    hidden(0)
    hidden(1)
    load_down.wait()
    for s in range(2):
        for k in range(3):
            hid_wait(s, k)
    for d in (1, 2, 3):
        copy_wait(sendbuf.at[0, turn(d)], disp_send.at[0, d - 1])
    pl.loop(0, out_steps)(down)

    for s in range(2):

        @pl.when(goes[s])
        def _():
            copy_wait(states[s], hi_send.at[s])

        copy_wait(xbuf.at[s, 1], lo_send.at[s])
        pltpu.make_async_copy(xbuf.at[s, 0], homes[s], out_sem.at[s]).wait()
        copy_wait(rows_ref.at[s, pl.ds(c * 4, 4)], core_send.at[s])
        for k in range(3):
            copy_wait(hs.at[s, 0], hid_send.at[s, k])
    for d in (1, 2, 3):
        copy_wait(sendbuf.at[1, turn(d)], disp_send.at[1, d - 1])
    for k in range(3):
        copy_wait(wd.at[part], wd_send.at[k])
    for k in range(8):
        d, cc = k // 2, k % 2
        source = pl.ds(pl.multiple_of(((c + cc) % 2) * half, 128), half)
        copy_wait(returned.at[turn(4 - d), :, source], ret_recv.at[k])
        if k:
            copy_wait(sendbuf.at[0, turn(d), :, source], ret_send.at[k])


def finish_kernel(
    route_a, route_b, weight_a, weight_b, home_a, home_b, returned, new_a, new_b, sel_ref
):
    tok = route_a.shape[0]
    cap2 = returned.shape[1]
    cap = cap2 // 2
    slots = 4 * cap2

    @pl.when(pl.program_id(0) == 0)
    def _():
        tri = (iota((tok, tok), 1) < iota((tok, tok), 0)).astype(BF16)
        r = iota((tok, slots), 1)
        expert = sum((r >= cap2 * k).astype(jnp.int32) for k in range(1, 4))
        rem = r - expert * cap2
        stream = (rem >= cap).astype(jnp.int32)
        value = (expert * cap + rem - stream * cap).astype(F32)
        for s, route_ref in enumerate((route_a, route_b)):
            route = route_ref[...]
            onehot = (iota((tok, 128), 1) == route).astype(F32)
            earlier = jnp.dot(tri, onehot.astype(BF16), preferred_element_type=F32)
            rank = jnp.sum(onehot * earlier, axis=1, keepdims=True)
            target = route.astype(F32) * cap + rank
            sel_ref[s] = jnp.where((value == target) & (stream == s), 1.0, 0.0).astype(BF16)

    block = returned[...].reshape(slots, returned.shape[2])
    for s, (weight, home, new) in enumerate(
        ((weight_a, home_a, new_a), (weight_b, home_b, new_b))
    ):
        taken = jnp.dot(sel_ref[s], block, preferred_element_type=F32)
        new[...] = (home[...].astype(F32) + taken * weight[...]).astype(BF16)


def local(
    state_a,
    state_b,
    enter_a,
    enter_b,
    route_a,
    route_b,
    weight_a,
    weight_b,
    norm_gain,
    w_gate,
    w_up,
    w_down,
):
    tok, width = enter_a.shape
    sections = lax.axis_size("pp")
    experts = lax.axis_size("ep") // EGROUP
    cap = tok * 5 // (4 * experts)
    cap2 = 2 * cap
    half = width // 2
    share = w_gate.shape[1]
    send_steps = width // SEND_COLS
    out_steps = half // OUT_COLS
    routes = jnp.concatenate([route_a.reshape(1, tok), route_b.reshape(1, tok)], axis=0)
    hbm = pl.BlockSpec(memory_space=pl.ANY)
    vmem = pl.BlockSpec(memory_space=pltpu.VMEM)
    dma = pltpu.SemaphoreType.DMA
    home_a, home_b, returned = pl.pallas_call(
        functools.partial(relay_kernel, sections),
        out_shape=(
            jax.ShapeDtypeStruct((tok, width), BF16),
            jax.ShapeDtypeStruct((tok, width), BF16),
            jax.ShapeDtypeStruct((experts, cap2, width), BF16),
        ),
        in_specs=[vmem, vmem] + [hbm] * 7,
        out_specs=(hbm, hbm, hbm),
        scratch_shapes=[
            pltpu.VMEM((2, 2, tok, width), BF16),
            pltpu.VMEM((8, tok), F32),
            pltpu.VMEM((8, tok), F32),
            pltpu.VMEM((2 * tok, 128), F32),
            pltpu.VMEM((experts * cap2, 2 * tok), BF16),
            pltpu.VMEM((2, experts, cap2, width), BF16),
            pltpu.VMEM((2, 8, cap2, width), BF16),
            pltpu.VMEM((2 * share, width), BF16),
            pltpu.VMEM((EGROUP, share, half), BF16),
            pltpu.VMEM((8 * cap2, 2 * share), F32),
            pltpu.VMEM((2, 2, 8 * cap, share), BF16),
            pltpu.VMEM((2, EGROUP, 8 * cap, share), BF16),
            dma((3,)),
            dma((2,)),
            dma((2,)),
            dma((2, HOPS)),
            dma((2, HOPS)),
            dma((2,)),
            dma((2,)),
            dma((2, 3)),
            dma((2, 3, send_steps)),
            dma((2, send_steps)),
            dma((2,)),
            dma((2, send_steps)),
            dma((2, 3)),
            dma((2, 3)),
            dma((3,)),
            dma((3, out_steps)),
            dma((8,)),
            dma((8,)),
        ],
        compiler_params=pltpu.CompilerParams(
            collective_id=0, has_side_effects=True, vmem_limit_bytes=60 * 2**20
        ),
        name="relay",
    )(
        routes,
        norm_gain,
        state_a[0],
        state_b[0],
        enter_a,
        enter_b,
        w_gate[0],
        w_up[0],
        w_down[0],
    )
    cols = 1024
    whole = pl.BlockSpec((tok, 1), lambda j: (0, 0))
    piece = pl.BlockSpec((tok, cols), lambda j: (0, j))
    new_a, new_b = pl.pallas_call(
        finish_kernel,
        grid=(width // cols,),
        in_specs=[whole] * 4
        + [piece, piece, pl.BlockSpec((experts, cap2, cols), lambda j: (0, 0, j))],
        out_specs=(piece, piece),
        out_shape=(
            jax.ShapeDtypeStruct((tok, width), BF16),
            jax.ShapeDtypeStruct((tok, width), BF16),
        ),
        scratch_shapes=[pltpu.VMEM((2, tok, experts * cap2), BF16)],
        name="finish",
    )(route_a[0], route_b[0], weight_a[0], weight_b[0], home_a, home_b, returned)
    return (new_a[None], new_b[None])


def solution(mesh):
    return jax.shard_map(
        local,
        mesh=mesh,
        in_specs=(
            P("pp", "ep", None),
            P("pp", "ep", None),
            P("ep", None),
            P("ep", None),
            P("pp", "ep", None),
            P("pp", "ep", None),
            P("pp", "ep", None),
            P("pp", "ep", None),
            P("pp", None),
            P("pp", "ep", None),
            P("pp", "ep", None),
            P("pp", "ep", None),
        ),
        out_specs=(P("pp", "ep", None), P("pp", "ep", None)),
        check_vma=False,
    )
```

```python
import functools

import jax
import jax.numpy as jnp
from jax import lax
from jax.experimental import pallas as pl
from jax.experimental.pallas import tpu as pltpu
from jax.sharding import PartitionSpec as P

EGROUP = 4
MESH = pl.DeviceIdType.MESH
BF16 = jnp.bfloat16
F32 = jnp.float32

STEP = 1024
OUT_COLS = 256
LAG = 7
EARLY = 6
BEHIND = 2


def iota(shape, dim):
    return lax.broadcasted_iota(jnp.int32, shape, dim)


def copy_wait(ref, sem):
    pltpu.make_async_copy(ref, ref, sem).wait()


def relay_kernel(
    sections,
    meta_ref,
    gain_ref,
    state_a,
    state_b,
    enter_a,
    enter_b,
    w_gate,
    w_up,
    w_down,
    new_a,
    new_b,
    stage,
    stat,
    wide_ref,
    inv_col,
    xbuf,
    inv_ref,
    tgt_own,
    tgt_far,
    sel_ref,
    pick_ref,
    weight_ref,
    sendbuf,
    returned,
    rows_ref,
    wgu,
    wd,
    acc,
    hs,
    hid,
    local_sem,
    tgt_sems,
    stage_sem,
    inv_sems,
    hi_send,
    arr_sem,
    home_sem,
    lo_send,
    out_sem,
    disp_send,
    disp_recv,
    disp_local,
    core_send,
    core_recv,
    hid_send,
    hid_recv,
    wd_send,
    wd_recv,
    ret_send,
    ret_recv,
):
    tok, width = state_a.shape
    share = w_gate.shape[0]
    half = width // 2
    cap2 = sendbuf.shape[1]
    cap = cap2 // 2
    steps = width // STEP
    total = 2 * steps
    out_steps = half // OUT_COLS

    p = lax.axis_index("pp")
    ep = lax.axis_index("ep")
    y, z, c = ep // 4, (ep // 2) % 2, ep % 2
    odd = p % 2
    inner = (p % (sections - 1) + sections - 2) // (sections - 1)
    edge = inner == 0
    hop_to = (p + inner * (2 * odd - 1), p + 1 - 2 * odd)
    far = y * 4 + (1 - z) * 2 + c
    part = z * 2 + c

    def at(yy, zz, cc):
        return (p, yy * 4 + zz * 2 + cc)

    def turn(d):
        return (y + d) % 4

    def remote(src, dst, send, recv, device):
        return pltpu.make_async_remote_copy(
            src, dst, send, recv, device_id=device, device_id_type=MESH
        )

    def cols_of(i, size, base=0):
        return pl.ds(pl.multiple_of(base + i * size, 128), size)

    def staging(t, ref):
        return pltpu.make_async_copy(ref, stage.at[t], stage_sem.at[t])

    @pl.when(edge & (odd == 0))
    def _():
        staging(0, enter_a).start()

    @pl.when(edge & (odd == 1))
    def _():
        staging(0, enter_b).start()

    @pl.when((inner == 1) & (odd == 0))
    def _():
        staging(0, state_b).start()

    @pl.when((inner == 1) & (odd == 1))
    def _():
        staging(0, state_a).start()

    @pl.when(odd == 0)
    def _():
        staging(1, state_a).start()

    @pl.when(odd == 1)
    def _():
        staging(1, state_b).start()

    barrier = pltpu.get_barrier_semaphore()

    def greet(device):
        pl.semaphore_signal(barrier, inc=1, device_id=device, device_id_type=MESH)

    for d in range(4):
        for cc in range(2):
            if d or cc:
                greet(at(turn(d), z, (c + cc) % 2))
    greet(at(y, 1 - z, c))
    greet(at(y, 1 - z, 1 - c))
    greet((hop_to[1], far))

    @pl.when(inner == 1)
    def _():
        greet((hop_to[0], far))

    pl.semaphore_wait(barrier, 10 + inner)

    def hop(t, j):
        cols = cols_of(j, STEP)
        return remote(
            stage.at[t, :, cols],
            xbuf.at[t, 1, :, cols],
            hi_send.at[t],
            arr_sem.at[t, j],
            (hop_to[t], far),
        )

    def enter_here(j):
        cols = cols_of(j, STEP)
        return pltpu.make_async_copy(
            stage.at[0, :, cols], xbuf.at[0, 0, :, cols], home_sem.at[0, j]
        )

    def across(t, j):
        cols = cols_of(j, STEP)
        return remote(
            xbuf.at[t, 1, :, cols],
            xbuf.at[t, 0, :, cols],
            lo_send.at[t],
            home_sem.at[t, j],
            (p, far),
        )

    def inv_hop(t):
        return remote(
            stat.at[t], inv_ref.at[t, 1], inv_sems.at[t, 0], inv_sems.at[t, 1], (hop_to[t], far)
        )

    def inv_here():
        return pltpu.make_async_copy(stat.at[0], inv_ref.at[0, 0], inv_sems.at[0, 3])

    def inv_across(t):
        return remote(
            inv_ref.at[t, 1], inv_ref.at[t, 0], inv_sems.at[t, 2], inv_sems.at[t, 3], (p, far)
        )

    def depart(t):
        @pl.loop(0, tok // 16)
        def _(i):
            rows = pl.ds(pl.multiple_of(i * 16, 16), 16)
            block = stage[t, rows, :].astype(F32)
            mean = jnp.mean(block * block, axis=-1, keepdims=True)
            wide_ref[rows, :] = jnp.broadcast_to(lax.rsqrt(mean + 1e-06), (16, 128))

        same = iota((tok, tok), 1) == iota((tok, tok), 0)
        line = jnp.sum(jnp.where(same, wide_ref[...], 0.0), axis=0, keepdims=True)
        stat[t] = jnp.broadcast_to(line, (8, tok))
        inv_hop(t).start()

        @pl.loop(1, steps)
        def _(j):
            hop(t, j).start()

        if t == 0:

            @pl.when(edge)
            def _():
                inv_here().start()

                @pl.loop(0, steps)
                def _(j):
                    enter_here(j).start()

    def wd_other(k):
        return (z, 1 - c) if k == 0 else (1 - z, c if k == 1 else 1 - c)

    def wd_copy(k, n):
        zz, cc = wd_other(k)
        return remote(
            w_down.at[:, cols_of(n, OUT_COLS, cc * half)],
            wd.at[part, :, cols_of(n, OUT_COLS)],
            wd_send.at[k],
            wd_recv.at[k, n],
            at(y, zz, cc),
        )

    def wd_wait(k, n):
        zz, cc = wd_other(k)
        copy_wait(wd.at[zz * 2 + cc, :, cols_of(n, OUT_COLS)], wd_recv.at[k, n])

    for k in (1, 2, 0):
        wd_copy(k, 0).start()
    copy_wait(stage.at[0], stage_sem.at[0])
    hop(0, 0).start()

    tri = (iota((tok, tok), 0) < iota((tok, tok), 1)).astype(BF16)
    slot_rows = []
    for t in range(2):
        route = jnp.where(odd == t, meta_ref[0:1, :], meta_ref[1:2, :])
        onehot = (iota((16, tok), 0).astype(F32) == route).astype(F32)
        earlier = jnp.dot(onehot.astype(BF16), tri, preferred_element_type=F32)
        rank = jnp.sum(onehot * earlier, axis=0, keepdims=True)
        slot_rows.append(route * cap + rank)
    tgt_own[...] = jnp.concatenate(slot_rows + [jnp.zeros((6, tok), F32)], axis=0)
    tgt_copy = remote(tgt_own, tgt_far, tgt_sems.at[0], tgt_sems.at[1], (p, far))
    tgt_copy.start()
    depart(0)
    copy_wait(stage.at[1], stage_sem.at[1])
    hop(1, 0).start()
    depart(1)

    load_gate = pltpu.make_async_copy(w_gate, wgu.at[pl.ds(0, share)], local_sem.at[0])
    load_up = pltpu.make_async_copy(w_up, wgu.at[pl.ds(share, share)], local_sem.at[1])
    load_down = pltpu.make_async_copy(
        w_down.at[:, cols_of(c, half)], wd.at[part], local_sem.at[2]
    )
    load_gate.start()
    load_up.start()
    load_down.start()

    tgt_copy.wait()
    slots = 4 * cap2

    def slot_value(dim, shape):
        r = iota(shape, dim)
        expert = sum((r >= cap2 * k).astype(jnp.int32) for k in range(1, 4))
        rem = r - expert * cap2
        second = (rem >= cap).astype(jnp.int32)
        return (expert * cap + rem - second * cap).astype(F32), second

    def column(line):
        same = iota((tok, tok), 1) == iota((tok, tok), 0)
        lines = jnp.broadcast_to(line, (tok, tok))
        return jnp.sum(jnp.where(same, lines, 0.0), axis=1, keepdims=True)

    value, rel = slot_value(0, (slots, tok))
    lane_value, phase = slot_value(1, (tok, slots))
    for t in range(2):
        here = jnp.where((value == tgt_own[t : t + 1, :]) & (rel == 0), 1.0, 0.0)
        there = jnp.where((value == tgt_far[t : t + 1, :]) & (rel == 1), 1.0, 0.0)
        sel_ref[t] = jnp.concatenate([here, there], axis=1).astype(BF16)
        target = column(tgt_own[t : t + 1, :])
        picks = (lane_value == target) & (phase == t)
        pick_ref[t] = jnp.where(picks, 1.0, 0.0).astype(BF16)
        weight = jnp.where(odd == t, meta_ref[2:3, :], meta_ref[3:4, :])
        weight_ref[t] = jnp.broadcast_to(column(weight), (tok, 128))

    def disp(t, d, j):
        e = turn(d)
        cols = cols_of(j, STEP)
        return remote(
            sendbuf.at[e, :, cols],
            rows_ref.at[t, c * 4 + y, :, cols],
            disp_send.at[d - 1, j],
            disp_recv.at[t, d - 1, j],
            at(e, z, c),
        )

    def disp_left(j):
        for d in (1, 2, 3):
            copy_wait(sendbuf.at[turn(d), :, cols_of(j, STEP)], disp_send.at[d - 1, j])

    def disp_here(t, j):
        cols = cols_of(j, STEP)
        return pltpu.make_async_copy(
            sendbuf.at[y, :, cols], rows_ref.at[t, c * 4 + y, :, cols], disp_local.at[t, j]
        )

    def arrive(t, j):
        passed_on = (t == 1) | (inner == 1)
        copy_wait(xbuf.at[t, 1, :, cols_of(j, STEP)], arr_sem.at[t, j])

        @pl.when(passed_on)
        def _():
            across(t, j).start()

        @pl.when(j == 0)
        def _():
            copy_wait(inv_ref.at[t, 1], inv_sems.at[t, 1])

            @pl.when(passed_on)
            def _():
                inv_across(t).start()

    def dispatch(t, j):
        @pl.when(j == 0)
        def _():
            copy_wait(inv_ref.at[t, 0], inv_sems.at[t, 3])
            for side in range(2):
                inv_col[pl.ds(side * tok, tok), :] = jnp.broadcast_to(
                    column(inv_ref[t, side, 0:1, :]), (tok, 128)
                )

        copy_wait(xbuf.at[t, 0, :, cols_of(j, STEP)], home_sem.at[t, j])

        @pl.when(t == 1)
        def _():
            disp_left(j)

        for i in range(STEP // 512):
            cols = cols_of(i, 512, j * STEP)
            x = xbuf[t, :, :, cols].reshape(2 * tok, 512).astype(F32)
            normed = (x * inv_col[:, 0:1] * gain_ref[:, cols]).astype(BF16)
            picked = jnp.dot(sel_ref[t], normed, preferred_element_type=F32)
            sendbuf[:, :, cols] = picked.astype(BF16).reshape(4, cap2, 512)
        for d in (1, 3, 2):
            disp(t, d, j).start()
        disp_here(t, j).start()

    def cores(t, j):
        block = rows_ref.at[t, pl.ds(c * 4, 4), :, cols_of(j, STEP)]
        return remote(block, block, core_send.at[t], core_recv.at[t, j], at(y, z, 1 - c))

    def share_rows(t, j):
        for d in (1, 3, 2):
            copy_wait(
                rows_ref.at[t, c * 4 + turn(4 - d), :, cols_of(j, STEP)],
                disp_recv.at[t, d - 1, j],
            )
        disp_here(t, j).wait()
        cores(t, j).start()

    def project(t, j):
        cols = cols_of(j, STEP)
        copy_wait(rows_ref.at[t, pl.ds((1 - c) * 4, 4), :, cols], core_recv.at[t, j])

        @pl.when(j == 0)
        def _():
            acc[...] = jnp.zeros_like(acc)

        lhs = rows_ref[t, :, :, cols].reshape(8 * cap2, STEP)
        acc[...] += lax.dot_general(
            lhs, wgu[:, cols], (((1,), (1,)), ((), ())), preferred_element_type=F32
        )

        @pl.when(j == steps - 1)
        def _():
            hidden(t)

    def hid_copy(t, k):
        if k == 0:
            return remote(
                hs.at[t, 0], hid.at[t, part], hid_send.at[t, 0], hid_recv.at[t, 0], at(y, z, 1 - c)
            )
        if k == 1:
            return remote(
                hs.at[t, 1], hid.at[t, part], hid_send.at[t, 1], hid_recv.at[t, 1], (p, far)
            )
        block = hid.at[t, (1 - z) * 2 + c]
        return remote(block, block, hid_send.at[t, 2], hid_recv.at[t, 2], at(y, z, 1 - c))

    def hid_wait(t, k):
        zz, cc = ((z, 1 - c), (1 - z, c), (1 - z, 1 - c))[k]
        copy_wait(hid.at[t, zz * 2 + cc], hid_recv.at[t, k])

    def hidden(t):
        gate, up = acc[:, :share], acc[:, share:]
        h = gate / (1.0 + jnp.exp(-gate)) * up
        mine = [h[b * cap2 : b * cap2 + cap] for b in range(8)]
        others = [h[b * cap2 + cap : (b + 1) * cap2] for b in range(8)]
        hs[t, 1] = jnp.concatenate(others, axis=0).astype(BF16)
        hid_copy(t, 1).start()
        hs[t, 0] = jnp.concatenate(mine, axis=0).astype(BF16)
        hid_copy(t, 0).start()
        hid[t, part] = hs[t, 0]

    def send_down(lo, hi):
        @pl.loop(lo, hi)
        def _(n):
            for k in (1, 2, 0):
                wd_copy(k, n).start()

    load_gate.wait()
    load_up.wait()

    @pl.loop(0, total + LAG + 1)
    def _(k):
        @pl.when(k < total)
        def _():
            arrive(k // steps, k % steps)

        @pl.when(k == total - 1)
        def _():
            send_down(1, EARLY)

        @pl.when((k >= 1) & (k <= total))
        def _():
            dispatch((k - 1) // steps, (k - 1) % steps)

        @pl.when((k >= LAG) & (k < total + LAG))
        def _():
            share_rows((k - LAG) // steps, (k - LAG) % steps)

        @pl.when(k >= LAG + 1)
        def _():
            project((k - LAG - 1) // steps, (k - LAG - 1) % steps)

    send_down(EARLY, out_steps)
    for t in range(2):
        hid_wait(t, 1)
        hid_copy(t, 2).start()
    load_down.wait()
    pl.loop(0, steps)(disp_left)
    for t in range(2):
        hid_wait(t, 0)
        hid_wait(t, 2)

    def back(k, n):
        d, cc = k // 2, k % 2
        to = (c + cc) % 2
        src = sendbuf.at[turn(d), :, cols_of(n, OUT_COLS, to * half)]
        dst = returned.at[y, :, cols_of(n, OUT_COLS, c * half)]
        if k == 0:
            return pltpu.make_async_copy(src, dst, ret_recv.at[c, n])
        return remote(src, dst, ret_send.at[k], ret_recv.at[c, n], at(turn(d), z, to))

    def down(n):
        for k in range(3):
            wd_wait(k, n)
        cols = cols_of(n, OUT_COLS)
        outs = []
        for t in range(2):
            out = jnp.zeros((8 * cap, OUT_COLS), F32)
            for g in range(EGROUP):
                out += jnp.dot(hid[t, g], wd[g, :, cols], preferred_element_type=F32)
            outs.append(out)
        for cc in range(2):
            rows = []
            for b in range(4 * cc, 4 * cc + 4):
                rows += [out[b * cap : (b + 1) * cap] for out in outs]
            sendbuf[:, :, cols_of(n, OUT_COLS, cc * half)] = (
                jnp.concatenate(rows, axis=0).astype(BF16).reshape(4, cap2, OUT_COLS)
            )
        for k in (2, 3, 6, 7, 4, 5, 1, 0):
            back(k, n).start()

    def put(t, ref, side, n):
        cols = cols_of(n, OUT_COLS, side * half)
        return pltpu.make_async_copy(xbuf.at[t, 0, :, cols], ref.at[:, cols], out_sem.at[t])

    def finish(n):
        for side in range(2):
            cols = cols_of(n, OUT_COLS, side * half)
            copy_wait(returned.at[:, :, cols], ret_recv.at[side, n])
            block = returned[:, :, cols].reshape(slots, OUT_COLS)
            for t in range(2):
                taken = jnp.dot(pick_ref[t], block, preferred_element_type=F32)
                home = xbuf[t, 0, :, cols].astype(F32)
                xbuf[t, 0, :, cols] = (home + taken * weight_ref[t][:, 0:1]).astype(BF16)

                @pl.when(odd == t)
                def _():
                    put(t, new_a, side, n).start()

                @pl.when(odd != t)
                def _():
                    put(t, new_b, side, n).start()

    @pl.loop(0, out_steps + BEHIND)
    def _(n):
        @pl.when(n < out_steps)
        def _():
            down(n)

        @pl.when(n >= BEHIND)
        def _():
            finish(n - BEHIND)

    for t in range(2):
        copy_wait(stage.at[t], hi_send.at[t])
        copy_wait(stat.at[t], inv_sems.at[t, 0])

        @pl.when((t == 1) | (inner == 1))
        def _():
            copy_wait(xbuf.at[t, 1], lo_send.at[t])
            copy_wait(inv_ref.at[t, 1], inv_sems.at[t, 2])

        copy_wait(xbuf.at[t, 0], out_sem.at[t])
        copy_wait(rows_ref.at[t, pl.ds(c * 4, 4)], core_send.at[t])
        for k in range(3):
            copy_wait(hs.at[t, 0], hid_send.at[t, k])
    for k in range(3):
        copy_wait(wd.at[part], wd_send.at[k])
    for k in range(1, 8):
        d, cc = k // 2, k % 2
        copy_wait(
            sendbuf.at[turn(d), :, cols_of((c + cc) % 2, half)],
            ret_send.at[k],
        )


def local(
    state_a,
    state_b,
    enter_a,
    enter_b,
    route_a,
    route_b,
    weight_a,
    weight_b,
    norm_gain,
    w_gate,
    w_up,
    w_down,
):
    tok, width = enter_a.shape
    sections = lax.axis_size("pp")
    experts = lax.axis_size("ep") // EGROUP
    cap = tok * 5 // (4 * experts)
    cap2 = 2 * cap
    half = width // 2
    share = w_gate.shape[1]
    steps = width // STEP
    out_steps = half // OUT_COLS
    lines = [v.reshape(1, tok).astype(F32) for v in (route_a, route_b, weight_a, weight_b)]
    meta = jnp.concatenate(lines + [jnp.zeros((4, tok), F32)], axis=0)
    hbm = pl.BlockSpec(memory_space=pl.ANY)
    vmem = pl.BlockSpec(memory_space=pltpu.VMEM)
    dma = pltpu.SemaphoreType.DMA
    new_a, new_b = pl.pallas_call(
        functools.partial(relay_kernel, sections),
        out_shape=(
            jax.ShapeDtypeStruct((tok, width), BF16),
            jax.ShapeDtypeStruct((tok, width), BF16),
        ),
        in_specs=[vmem, vmem] + [hbm] * 7,
        out_specs=(hbm, hbm),
        scratch_shapes=[
            pltpu.VMEM((2, tok, width), BF16),
            pltpu.VMEM((2, 8, tok), F32),
            pltpu.VMEM((tok, 128), F32),
            pltpu.VMEM((2 * tok, 128), F32),
            pltpu.VMEM((2, 2, tok, width), BF16),
            pltpu.VMEM((2, 2, 8, tok), F32),
            pltpu.VMEM((8, tok), F32),
            pltpu.VMEM((8, tok), F32),
            pltpu.VMEM((2, experts * cap2, 2 * tok), BF16),
            pltpu.VMEM((2, tok, experts * cap2), BF16),
            pltpu.VMEM((2, tok, 128), F32),
            pltpu.VMEM((experts, cap2, width), BF16),
            pltpu.VMEM((experts, cap2, width), BF16),
            pltpu.VMEM((2, 8, cap2, width), BF16),
            pltpu.VMEM((2 * share, width), BF16),
            pltpu.VMEM((EGROUP, share, half), BF16),
            pltpu.VMEM((8 * cap2, 2 * share), F32),
            pltpu.VMEM((2, 2, 8 * cap, share), BF16),
            pltpu.VMEM((2, EGROUP, 8 * cap, share), BF16),
            dma((3,)),
            dma((2,)),
            dma((2,)),
            dma((2, 4)),
            dma((2,)),
            dma((2, steps)),
            dma((2, steps)),
            dma((2,)),
            dma((2,)),
            dma((3, steps)),
            dma((2, 3, steps)),
            dma((2, steps)),
            dma((2,)),
            dma((2, steps)),
            dma((2, 3)),
            dma((2, 3)),
            dma((3,)),
            dma((3, out_steps)),
            dma((8,)),
            dma((2, out_steps)),
        ],
        compiler_params=pltpu.CompilerParams(
            collective_id=0, has_side_effects=True, vmem_limit_bytes=60 * 2**20
        ),
        name="relay",
    )(
        meta,
        norm_gain,
        state_a[0],
        state_b[0],
        enter_a,
        enter_b,
        w_gate[0],
        w_up[0],
        w_down[0],
    )
    return (new_a[None], new_b[None])


def solution(mesh):
    return jax.shard_map(
        local,
        mesh=mesh,
        in_specs=(
            P("pp", "ep", None),
            P("pp", "ep", None),
            P("ep", None),
            P("ep", None),
            P("pp", "ep", None),
            P("pp", "ep", None),
            P("pp", "ep", None),
            P("pp", "ep", None),
            P("pp", None),
            P("pp", "ep", None),
            P("pp", "ep", None),
            P("pp", "ep", None),
        ),
        out_specs=(P("pp", "ep", None), P("pp", "ep", None)),
        check_vma=False,
    )
```

```python
import functools

import jax
import jax.numpy as jnp
from jax import lax
from jax.experimental import pallas as pl
from jax.experimental.pallas import tpu as pltpu
from jax.sharding import PartitionSpec as P

EGROUP = 4
MESH = pl.DeviceIdType.MESH
BF16 = jnp.bfloat16
F32 = jnp.float32

STEP = 512
OUT_COLS = 256
LAG = 14
EARLY = 8
BEHIND = 2
AHEAD = 4
NEXT = 3
FILL = (10,)


def iota(shape, dim):
    return lax.broadcasted_iota(jnp.int32, shape, dim)


def copy_wait(ref, sem):
    pltpu.make_async_copy(ref, ref, sem).wait()


def relay_kernel(
    sections,
    route_a_in,
    route_b_in,
    weight_a_in,
    weight_b_in,
    gain_in,
    state_a,
    state_b,
    enter_a,
    enter_b,
    w_gate,
    w_up,
    w_down,
    news,
    route_a,
    route_b,
    weight_a,
    weight_b,
    gain_ref,
    stage,
    stat,
    wide_ref,
    inv_col,
    xbuf,
    inv_ref,
    tgt_own,
    tgt_far,
    sel_ref,
    pick_ref,
    weight_ref,
    sendbuf,
    outbuf,
    returned,
    rows_ref,
    wgu,
    wd,
    acc,
    hs,
    hid,
    local_sem,
    tgt_sems,
    stage_sem,
    inv_sems,
    hi_send,
    arr_sem,
    home_sem,
    lo_send,
    out_sem,
    disp_send,
    disp_recv,
    disp_local,
    core_send,
    core_recv,
    hid_send,
    hid_recv,
    wd_send,
    wd_recv,
    ret_send,
    ret_recv,
):
    tok, width = state_a.shape
    share = w_gate.shape[0]
    half = width // 2
    cap2 = sendbuf.shape[2]
    cap = cap2 // 2
    steps = width // STEP
    total = 2 * steps
    out_steps = half // OUT_COLS

    p = lax.axis_index("pp")
    ep = lax.axis_index("ep")
    y, z, c = ep // 4, (ep // 2) % 2, ep % 2
    odd = p % 2
    inner = (p % (sections - 1) + sections - 2) // (sections - 1)
    edge = inner == 0
    hop_to = (p + inner * (2 * odd - 1), p + 1 - 2 * odd)
    far = y * 4 + (1 - z) * 2 + c
    part = z * 2 + c

    def at(yy, zz, cc):
        return (p, yy * 4 + zz * 2 + cc)

    def turn(d):
        return (y + d) % 4

    def remote(src, dst, send, recv, device):
        return pltpu.make_async_remote_copy(
            src, dst, send, recv, device_id=device, device_id_type=MESH
        )

    def cols_of(i, size, base=0):
        return pl.ds(pl.multiple_of(base + i * size, 128), size)

    barrier = pltpu.get_barrier_semaphore()

    def greet(device):
        pl.semaphore_signal(barrier, inc=1, device_id=device, device_id_type=MESH)

    for d in range(4):
        for cc in range(2):
            if d or cc:
                greet(at(turn(d), z, (c + cc) % 2))
    greet(at(y, 1 - z, c))
    greet(at(y, 1 - z, 1 - c))
    greet((hop_to[1], far))

    @pl.when(inner == 1)
    def _():
        greet((hop_to[0], far))

    def staging(t, ref):
        @pl.loop(0, steps)
        def _(j):
            pltpu.make_async_copy(ref.at[:, cols_of(j, STEP)], stage.at[t, j], stage_sem.at[t]).start()

    @pl.when(edge & (odd == 0))
    def _():
        staging(0, enter_a)

    @pl.when(edge & (odd == 1))
    def _():
        staging(0, enter_b)

    @pl.when((inner == 1) & (odd == 0))
    def _():
        staging(0, state_b)

    @pl.when((inner == 1) & (odd == 1))
    def _():
        staging(0, state_a)

    small = [
        pltpu.make_async_copy(src, dst, local_sem.at[3 + i])
        for i, (src, dst) in enumerate(
            (
                (route_a_in, route_a),
                (route_b_in, route_b),
                (weight_a_in, weight_a),
                (weight_b_in, weight_b),
                (gain_in, gain_ref),
            )
        )
    ]
    for copy in small:
        copy.start()
    pl.semaphore_wait(barrier, 10 + inner)

    def hop(t, j):
        return remote(
            stage.at[t, j], xbuf.at[t, 1, j], hi_send.at[t], arr_sem.at[t, j], (hop_to[t], far)
        )

    def enter_here(j):
        return pltpu.make_async_copy(stage.at[0, j], xbuf.at[0, 0, j], home_sem.at[0, j])

    def across(t, j):
        return remote(
            xbuf.at[t, 1, j], xbuf.at[t, 0, j], lo_send.at[t], home_sem.at[t, j], (p, far)
        )

    def inv_hop(t):
        return remote(
            stat.at[t], inv_ref.at[t, 1], inv_sems.at[t, 0], inv_sems.at[t, 1], (hop_to[t], far)
        )

    def inv_here():
        return pltpu.make_async_copy(stat.at[0], inv_ref.at[0, 0], inv_sems.at[0, 3])

    def inv_across(t):
        return remote(
            inv_ref.at[t, 1], inv_ref.at[t, 0], inv_sems.at[t, 2], inv_sems.at[t, 3], (p, far)
        )

    def depart(t):
        wide_ref[...] = jnp.zeros_like(wide_ref)

        @pl.loop(0, steps)
        def _(j):
            for i in range(STEP // 128):
                block = stage[t, j, :, i * 128 : (i + 1) * 128].astype(F32)
                wide_ref[...] += block * block

        mean = jnp.sum(wide_ref[...], axis=1, keepdims=True) * (1.0 / width)
        same = iota((tok, tok), 1) == iota((tok, tok), 0)
        line = jnp.sum(jnp.where(same, lax.rsqrt(mean + 1e-06), 0.0), axis=0, keepdims=True)
        stat[t] = jnp.broadcast_to(line, (8, tok))
        inv_hop(t).start()

        @pl.loop(2 - t, steps)
        def _(j):
            hop(t, j).start()

        if t == 0:

            @pl.when(edge)
            def _():
                inv_here().start()

                @pl.loop(0, steps)
                def _(j):
                    enter_here(j).start()

    def wd_other(k):
        return (z, 1 - c) if k == 0 else (1 - z, c if k == 1 else 1 - c)

    pair = 2 * OUT_COLS
    pairs = out_steps // 2

    def wd_copy(k, m):
        zz, cc = wd_other(k)
        return remote(
            w_down.at[:, cols_of(m, pair, cc * half)],
            wd.at[part, m],
            wd_send.at[k],
            wd_recv.at[k, m],
            at(y, zz, cc),
        )

    def wd_copy_last(k, i):
        zz, cc = wd_other(k)
        return remote(
            w_down.at[:, cols_of(out_steps - 2 + i, OUT_COLS, cc * half)],
            wd.at[part, pairs - 1, :, i * OUT_COLS : (i + 1) * OUT_COLS],
            wd_send.at[k],
            wd_recv.at[k, pairs - 1 + i],
            at(y, zz, cc),
        )

    def wd_wait(k, n):
        zz, cc = wd_other(k)

        @pl.when((n % 2 == 0) & (n < out_steps - 2))
        def _():
            copy_wait(wd.at[zz * 2 + cc, n // 2], wd_recv.at[k, n // 2])

        for i in range(2):

            @pl.when(n == out_steps - 2 + i)
            def _():
                block = wd.at[zz * 2 + cc, pairs - 1, :, i * OUT_COLS : (i + 1) * OUT_COLS]
                copy_wait(block, wd_recv.at[k, pairs - 1 + i])

    for k in (1, 0):
        wd_copy(k, 0).start()
    copy_wait(stage.at[0], stage_sem.at[0])
    hop(0, 0).start()
    hop(0, 1).start()
    @pl.when(odd == 0)
    def _():
        staging(1, state_a)

    @pl.when(odd == 1)
    def _():
        staging(1, state_b)

    for copy in small:
        copy.wait()
    tri = (iota((tok, tok), 0) < iota((tok, tok), 1)).astype(BF16)
    slot_rows = []
    for t in range(2):
        route = jnp.where(odd == t, route_a[...], route_b[...]).astype(F32)
        onehot = (iota((16, tok), 0).astype(F32) == route).astype(F32)
        earlier = jnp.dot(onehot.astype(BF16), tri, preferred_element_type=F32)
        rank = jnp.sum(onehot * earlier, axis=0, keepdims=True)
        slot_rows.append(route * cap + rank)
    tgt_own[...] = jnp.concatenate(slot_rows + [jnp.zeros((6, tok), F32)], axis=0)
    tgt_copy = remote(tgt_own, tgt_far, tgt_sems.at[0], tgt_sems.at[1], (p, far))
    tgt_copy.start()
    depart(0)
    copy_wait(stage.at[1], stage_sem.at[1])
    hop(1, 0).start()
    depart(1)

    load_gate = pltpu.make_async_copy(w_gate, wgu.at[pl.ds(0, share)], local_sem.at[0])
    load_up = pltpu.make_async_copy(w_up, wgu.at[pl.ds(share, share)], local_sem.at[1])
    load_gate.start()
    load_up.start()

    @pl.loop(0, out_steps // 2)
    def _(m):
        pltpu.make_async_copy(
            w_down.at[:, cols_of(m, 2 * OUT_COLS, c * half)], wd.at[part, m], local_sem.at[2]
        ).start()

    tgt_copy.wait()
    slots = 4 * cap
    r = iota((2 * slots, tok), 0)
    expert = sum((r >= cap2 * k).astype(jnp.int32) for k in range(1, 4))
    rem = r - expert * cap2
    rel = (rem >= cap).astype(jnp.int32)
    value = (expert * cap + rem - rel * cap).astype(F32)

    def column(line):
        same = iota((tok, tok), 1) == iota((tok, tok), 0)
        lines = jnp.broadcast_to(line, (tok, tok))
        return jnp.sum(jnp.where(same, lines, 0.0), axis=1, keepdims=True)

    for t in range(2):
        here = jnp.where((value == tgt_own[t : t + 1, :]) & (rel == 0), 1.0, 0.0)
        there = jnp.where((value == tgt_far[t : t + 1, :]) & (rel == 1), 1.0, 0.0)
        sel_ref[t] = jnp.concatenate([here, there], axis=1).astype(BF16)
        target = column(tgt_own[t : t + 1, :])
        picks = iota((tok, slots), 1).astype(F32) == target
        pick_ref[t] = jnp.where(picks, 1.0, 0.0).astype(BF16)
        weight = jnp.where(odd == t, weight_a[...], weight_b[...])
        weight_ref[t] = jnp.broadcast_to(column(weight), (tok, 128))

    def disp(t, d, j):
        e = turn(d)
        return remote(
            sendbuf.at[j, e],
            rows_ref.at[t, j, c * 4 + y],
            disp_send.at[d - 1, j],
            disp_recv.at[t, d - 1, j],
            at(e, z, c),
        )

    def disp_left(j):
        for d in (1, 2, 3):
            copy_wait(sendbuf.at[j, turn(d)], disp_send.at[d - 1, j])

    def disp_here(t, j):
        return pltpu.make_async_copy(
            sendbuf.at[j, y], rows_ref.at[t, j, c * 4 + y], disp_local.at[t, j]
        )

    def arrive(t, j):
        passed_on = (t == 1) | (inner == 1)
        copy_wait(xbuf.at[t, 1, j], arr_sem.at[t, j])

        @pl.when(passed_on)
        def _():
            across(t, j).start()

        @pl.when(j == 0)
        def _():
            copy_wait(inv_ref.at[t, 1], inv_sems.at[t, 1])

            @pl.when(passed_on)
            def _():
                inv_across(t).start()

    def dispatch(t, j):
        @pl.when(j == 0)
        def _():
            copy_wait(inv_ref.at[t, 0], inv_sems.at[t, 3])
            for side in range(2):
                inv_col[pl.ds(side * tok, tok), :] = jnp.broadcast_to(
                    column(inv_ref[t, side, 0:1, :]), (tok, 128)
                )

        copy_wait(xbuf.at[t, 0, j], home_sem.at[t, j])

        @pl.when(t == 1)
        def _():
            disp_left(j)

        x = xbuf[t, :, j].reshape(2 * tok, STEP).astype(F32)
        normed = (x * inv_col[:, 0:1] * gain_ref[:, cols_of(j, STEP)]).astype(BF16)
        picked = jnp.dot(sel_ref[t], normed, preferred_element_type=F32)
        sendbuf[j] = picked.astype(BF16).reshape(4, cap2, STEP)
        for d in (1, 3, 2):
            disp(t, d, j).start()
        disp_here(t, j).start()

    def cores(t, j):
        block = rows_ref.at[t, j, pl.ds(c * 4, 4)]
        return remote(block, block, core_send.at[t], core_recv.at[t, j], at(y, z, 1 - c))

    def share_rows(t, j):
        for d in (1, 3, 2):
            copy_wait(rows_ref.at[t, j, c * 4 + turn(4 - d)], disp_recv.at[t, d - 1, j])
        disp_here(t, j).wait()
        cores(t, j).start()

    def project(t, j):
        cols = cols_of(j, STEP)
        copy_wait(rows_ref.at[t, j, pl.ds((1 - c) * 4, 4)], core_recv.at[t, j])

        @pl.when(j == 0)
        def _():
            acc[...] = jnp.zeros_like(acc)

        lhs = rows_ref[t, j].reshape(8 * cap2, STEP)
        acc[...] += lax.dot_general(
            lhs, wgu[:, cols], (((1,), (1,)), ((), ())), preferred_element_type=F32
        )

        @pl.when(j == steps - 1)
        def _():
            hidden(t)

    def hid_copy(t, k):
        if k == 0:
            return remote(
                hs.at[t, 0], hid.at[t, part], hid_send.at[t, 0], hid_recv.at[t, 0], at(y, z, 1 - c)
            )
        if k == 1:
            return remote(
                hs.at[t, 1], hid.at[t, part], hid_send.at[t, 1], hid_recv.at[t, 1], (p, far)
            )
        block = hid.at[t, (1 - z) * 2 + c]
        return remote(block, block, hid_send.at[t, 2], hid_recv.at[t, 2], at(y, z, 1 - c))

    def hid_wait(t, k):
        zz, cc = ((z, 1 - c), (1 - z, c), (1 - z, 1 - c))[k]
        copy_wait(hid.at[t, zz * 2 + cc], hid_recv.at[t, k])

    def hidden(t):
        gate, up = acc[:, :share], acc[:, share:]
        h = gate / (1.0 + jnp.exp(-gate)) * up
        mine = [h[b * cap2 : b * cap2 + cap] for b in range(8)]
        others = [h[b * cap2 + cap : (b + 1) * cap2] for b in range(8)]
        hs[t, 1] = jnp.concatenate(others, axis=0).astype(BF16)
        hid_copy(t, 1).start()
        hs[t, 0] = jnp.concatenate(mine, axis=0).astype(BF16)
        hid_copy(t, 0).start()
        hid[t, part] = hs[t, 0]

    def send_down(lo, hi):
        @pl.loop(lo, hi)
        def _(m):
            for k in (1, 2, 0):
                wd_copy(k, m).start()

    def send_down_rest():
        send_down(EARLY // 2, pairs - 1)
        for i in range(2):
            for k in (1, 2, 0):
                wd_copy_last(k, i).start()

    def back(t, k, n):
        d, cc = k // 2, k % 2
        to = (c + cc) % 2
        src = outbuf.at[t, n, to * 4 + turn(d)]
        dst = returned.at[t, n, c, y]
        if k == 0:
            return pltpu.make_async_copy(src, dst, ret_recv.at[t, c, n])
        return remote(src, dst, ret_send.at[t, k], ret_recv.at[t, c, n], at(turn(d), z, to))

    def down_wait(n):
        for k in range(3):
            wd_wait(k, n)

    def down(t, n):
        cols = cols_of(n % 2, OUT_COLS)
        out = jnp.zeros((8 * cap, OUT_COLS), F32)
        for g in range(EGROUP):
            out += jnp.dot(hid[t, g], wd[g, n // 2, :, cols], preferred_element_type=F32)
        outbuf[t, n] = out.reshape(8, cap, OUT_COLS).astype(BF16)
        for k in (2, 3, 6, 7, 4, 5, 1, 0):
            back(t, k, n).start()

    def pass_hidden(t):
        hid_wait(t, 1)
        hid_copy(t, 2).start()

    def have_hidden(t):
        hid_wait(t, 0)
        hid_wait(t, 2)

    def place(side, n):
        at_step = n // (STEP // OUT_COLS)
        return side * (half // STEP) + at_step, cols_of(n % (STEP // OUT_COLS), OUT_COLS)

    def put(t, side, n):
        j, cols = place(side, n)
        return pltpu.make_async_copy(
            xbuf.at[t, 0, j, :, cols],
            news.at[(t + odd) % 2, :, cols_of(n, OUT_COLS, side * half)],
            out_sem.at[t],
        )

    def finish(n):
        for side in range(2):
            j, cols = place(side, n)
            for t in range(2):
                copy_wait(returned.at[t, n, side], ret_recv.at[t, side, n])
                block = returned[t, n, side].astype(F32).reshape(slots, OUT_COLS)
                taken = jnp.dot(pick_ref[t], block.astype(BF16), preferred_element_type=F32)
                home = xbuf[t, 0, j, :, cols].astype(F32)
                xbuf[t, 0, j, :, cols] = (home + taken * weight_ref[t][:, 0:1]).astype(BF16)
                put(t, side, n).start()

    load_gate.wait()
    load_up.wait()
    copy_wait(wd.at[part], local_sem.at[2])

    @pl.loop(0, total + LAG + 1)
    def _(k):
        @pl.when(k < total)
        def _():
            arrive(k // steps, k % steps)

        @pl.when((k >= NEXT) & (k < total + NEXT))
        def _():
            dispatch((k - NEXT) // steps, (k - NEXT) % steps)

        @pl.when((k >= LAG) & (k < total + LAG))
        def _():
            share_rows((k - LAG) // steps, (k - LAG) % steps)

        @pl.when(k >= LAG + 1)
        def _():
            project((k - LAG - 1) // steps, (k - LAG - 1) % steps)

        @pl.when(k == 2)
        def _():
            wd_copy(2, 0).start()

        for n, when in enumerate(FILL, 1):

            @pl.when(k == when)
            def _():
                send_down(n, n + 1)

        @pl.when(k == steps + LAG)
        def _():
            send_down(1 + len(FILL), EARLY // 2)

        @pl.when(k == total + LAG - AHEAD - 2)
        def _():
            pass_hidden(0)

        @pl.when(k == total + LAG - AHEAD)
        def _():
            have_hidden(0)

        @pl.when((k >= total + LAG - AHEAD) & (k < total + LAG))
        def _():
            down_wait(k - (total + LAG - AHEAD))
            down(0, k - (total + LAG - AHEAD))

    send_down_rest()

    @pl.loop(AHEAD, EARLY - 1)
    def _(n):
        down_wait(n)
        down(0, n)

    pass_hidden(1)
    down_wait(EARLY - 1)
    down(0, EARLY - 1)
    have_hidden(1)

    @pl.loop(0, out_steps + BEHIND)
    def _(n):
        @pl.when(n < out_steps)
        def _():
            down(1, n)

        @pl.when((n >= EARLY - 1) & (n < out_steps - 1))
        def _():
            down_wait(n + 1)
            down(0, n + 1)

        @pl.when(n >= BEHIND)
        def _():
            finish(n - BEHIND)

    for t in range(2):
        copy_wait(stage.at[t], hi_send.at[t])
        copy_wait(stat.at[t], inv_sems.at[t, 0])

        @pl.when((t == 1) | (inner == 1))
        def _():
            copy_wait(xbuf.at[t, 1], lo_send.at[t])
            copy_wait(inv_ref.at[t, 1], inv_sems.at[t, 2])

        copy_wait(xbuf.at[t, 0], out_sem.at[t])
        copy_wait(rows_ref.at[t, :, pl.ds(c * 4, 4)], core_send.at[t])
        for k in range(3):
            copy_wait(hs.at[t, 0], hid_send.at[t, k])
    for k in range(3):
        copy_wait(wd.at[part], wd_send.at[k])
    pl.loop(0, steps)(disp_left)
    for t in range(2):
        for k in range(1, 8):
            d, cc = k // 2, k % 2
            copy_wait(outbuf.at[t, :, ((c + cc) % 2) * 4 + turn(d)], ret_send.at[t, k])


def local(
    state_a,
    state_b,
    enter_a,
    enter_b,
    route_a,
    route_b,
    weight_a,
    weight_b,
    norm_gain,
    w_gate,
    w_up,
    w_down,
):
    tok, width = enter_a.shape
    sections = lax.axis_size("pp")
    experts = lax.axis_size("ep") // EGROUP
    cap = tok * 5 // (4 * experts)
    cap2 = 2 * cap
    half = width // 2
    share = w_gate.shape[1]
    steps = width // STEP
    out_steps = half // OUT_COLS
    lines = [v.reshape(1, tok) for v in (route_a, route_b, weight_a, weight_b)]
    hbm = pl.BlockSpec(memory_space=pl.ANY)
    dma = pltpu.SemaphoreType.DMA
    news = pl.pallas_call(
        functools.partial(relay_kernel, sections),
        out_shape=jax.ShapeDtypeStruct((2, tok, width), BF16),
        in_specs=[hbm] * 12,
        out_specs=hbm,
        scratch_shapes=[
            pltpu.VMEM((1, tok), jnp.int32),
            pltpu.VMEM((1, tok), jnp.int32),
            pltpu.VMEM((1, tok), F32),
            pltpu.VMEM((1, tok), F32),
            pltpu.VMEM((1, width), F32),
            pltpu.VMEM((2, steps, tok, STEP), BF16),
            pltpu.VMEM((2, 8, tok), F32),
            pltpu.VMEM((tok, 128), F32),
            pltpu.VMEM((2 * tok, 128), F32),
            pltpu.VMEM((2, 2, steps, tok, STEP), BF16),
            pltpu.VMEM((2, 2, 8, tok), F32),
            pltpu.VMEM((8, tok), F32),
            pltpu.VMEM((8, tok), F32),
            pltpu.VMEM((2, experts * cap2, 2 * tok), BF16),
            pltpu.VMEM((2, tok, experts * cap), BF16),
            pltpu.VMEM((2, tok, 128), F32),
            pltpu.VMEM((steps, experts, cap2, STEP), BF16),
            pltpu.VMEM((2, out_steps, 8, cap, OUT_COLS), BF16),
            pltpu.VMEM((2, out_steps, 2, experts, cap, OUT_COLS), BF16),
            pltpu.VMEM((2, steps, 8, cap2, STEP), BF16),
            pltpu.VMEM((2 * share, width), BF16),
            pltpu.VMEM((EGROUP, out_steps // 2, share, 2 * OUT_COLS), BF16),
            pltpu.VMEM((8 * cap2, 2 * share), F32),
            pltpu.VMEM((2, 2, 8 * cap, share), BF16),
            pltpu.VMEM((2, EGROUP, 8 * cap, share), BF16),
            dma((8,)),
            dma((2,)),
            dma((2,)),
            dma((2, 4)),
            dma((2,)),
            dma((2, steps)),
            dma((2, steps)),
            dma((2,)),
            dma((2,)),
            dma((3, steps)),
            dma((2, 3, steps)),
            dma((2, steps)),
            dma((2,)),
            dma((2, steps)),
            dma((2, 3)),
            dma((2, 3)),
            dma((3,)),
            dma((3, out_steps // 2 + 1)),
            dma((2, 8)),
            dma((2, 2, out_steps)),
        ],
        compiler_params=pltpu.CompilerParams(
            collective_id=0, has_side_effects=True, vmem_limit_bytes=62 * 2**20
        ),
        name="relay",
    )(
        *lines,
        norm_gain,
        state_a[0],
        state_b[0],
        enter_a,
        enter_b,
        w_gate[0],
        w_up[0],
        w_down[0],
    )
    return (news[0:1], news[1:2])


def solution(mesh):
    return jax.shard_map(
        local,
        mesh=mesh,
        in_specs=(
            P("pp", "ep", None),
            P("pp", "ep", None),
            P("ep", None),
            P("ep", None),
            P("pp", "ep", None),
            P("pp", "ep", None),
            P("pp", "ep", None),
            P("pp", "ep", None),
            P("pp", None),
            P("pp", "ep", None),
            P("pp", "ep", None),
            P("pp", "ep", None),
        ),
        out_specs=(P("pp", "ep", None), P("pp", "ep", None)),
        check_vma=False,
    )
```

```python
import functools

import jax
import jax.numpy as jnp
from jax import lax
from jax.experimental import pallas as pl
from jax.experimental.pallas import tpu as pltpu
from jax.sharding import PartitionSpec as P

EGROUP = 4
MESH = pl.DeviceIdType.MESH
BF16 = jnp.bfloat16
F32 = jnp.float32

STEP = 512
OUT_COLS = 256
LAG = 14
EARLY = 8
AHEAD = 4
NEXT = 3
FILL = (10,)


def iota(shape, dim):
    return lax.broadcasted_iota(jnp.int32, shape, dim)


def copy_wait(ref, sem):
    pltpu.make_async_copy(ref, ref, sem).wait()


def relay_kernel(
    sections,
    route_a_in,
    route_b_in,
    weight_a_in,
    weight_b_in,
    gain_in,
    state_a,
    state_b,
    enter_a,
    enter_b,
    w_gate,
    w_up,
    w_down,
    news,
    route_a,
    route_b,
    weight_a,
    weight_b,
    gain_ref,
    stage,
    stat,
    wide_ref,
    inv_col,
    xbuf,
    inv_ref,
    tgt_own,
    tgt_far,
    sel_ref,
    pick_ref,
    weight_ref,
    sendbuf,
    outbuf,
    returned,
    rows_ref,
    wgu,
    wd,
    acc,
    hs,
    hid,
    local_sem,
    tgt_sems,
    stage_sem,
    inv_sems,
    hi_send,
    arr_sem,
    home_sem,
    lo_send,
    out_sem,
    disp_send,
    disp_recv,
    disp_local,
    core_send,
    core_recv,
    hid_send,
    hid_recv,
    wd_send,
    wd_recv,
    ret_send,
    ret_recv,
):
    tok, width = state_a.shape
    share = w_gate.shape[0]
    half = width // 2
    cap2 = sendbuf.shape[2]
    cap = cap2 // 2
    steps = width // STEP
    total = 2 * steps
    out_steps = half // OUT_COLS

    p = lax.axis_index("pp")
    ep = lax.axis_index("ep")
    y, z, c = ep // 4, (ep // 2) % 2, ep % 2
    odd = p % 2
    inner = (p % (sections - 1) + sections - 2) // (sections - 1)
    edge = inner == 0
    hop_to = (p + inner * (2 * odd - 1), p + 1 - 2 * odd)
    far = y * 4 + (1 - z) * 2 + c
    part = z * 2 + c

    def at(yy, zz, cc):
        return (p, yy * 4 + zz * 2 + cc)

    def turn(d):
        return (y + d) % 4

    def remote(src, dst, send, recv, device):
        return pltpu.make_async_remote_copy(
            src, dst, send, recv, device_id=device, device_id_type=MESH
        )

    def cols_of(i, size, base=0):
        return pl.ds(pl.multiple_of(base + i * size, 128), size)

    barrier = pltpu.get_barrier_semaphore()

    def greet(device):
        pl.semaphore_signal(barrier, inc=1, device_id=device, device_id_type=MESH)

    for d in range(4):
        for cc in range(2):
            if d or cc:
                greet(at(turn(d), z, (c + cc) % 2))
    greet(at(y, 1 - z, c))
    greet(at(y, 1 - z, 1 - c))
    greet((hop_to[1], far))

    @pl.when(inner == 1)
    def _():
        greet((hop_to[0], far))

    def staging(t, ref):
        @pl.loop(0, steps)
        def _(j):
            pltpu.make_async_copy(ref.at[:, cols_of(j, STEP)], stage.at[t, j], stage_sem.at[t]).start()

    @pl.when(edge & (odd == 0))
    def _():
        staging(0, enter_a)

    @pl.when(edge & (odd == 1))
    def _():
        staging(0, enter_b)

    @pl.when((inner == 1) & (odd == 0))
    def _():
        staging(0, state_b)

    @pl.when((inner == 1) & (odd == 1))
    def _():
        staging(0, state_a)

    small = [
        pltpu.make_async_copy(src, dst, local_sem.at[3 + i])
        for i, (src, dst) in enumerate(
            (
                (route_a_in, route_a),
                (route_b_in, route_b),
                (weight_a_in, weight_a),
                (weight_b_in, weight_b),
                (gain_in, gain_ref),
            )
        )
    ]
    for copy in small:
        copy.start()
    pl.semaphore_wait(barrier, 10 + inner)

    def hop(t, j):
        return remote(
            stage.at[t, j], xbuf.at[t, 1, j], hi_send.at[t], arr_sem.at[t, j], (hop_to[t], far)
        )

    def enter_here(j):
        return pltpu.make_async_copy(stage.at[0, j], xbuf.at[0, 0, j], home_sem.at[0, j])

    def across(t, j):
        return remote(
            xbuf.at[t, 1, j], xbuf.at[t, 0, j], lo_send.at[t], home_sem.at[t, j], (p, far)
        )

    def inv_hop(t):
        return remote(
            stat.at[t], inv_ref.at[t, 1], inv_sems.at[t, 0], inv_sems.at[t, 1], (hop_to[t], far)
        )

    def inv_here():
        return pltpu.make_async_copy(stat.at[0], inv_ref.at[0, 0], inv_sems.at[0, 3])

    def inv_across(t):
        return remote(
            inv_ref.at[t, 1], inv_ref.at[t, 0], inv_sems.at[t, 2], inv_sems.at[t, 3], (p, far)
        )

    def depart(t):
        wide_ref[...] = jnp.zeros_like(wide_ref)

        @pl.loop(0, steps)
        def _(j):
            for i in range(STEP // 128):
                block = stage[t, j, :, i * 128 : (i + 1) * 128].astype(F32)
                wide_ref[...] += block * block

        mean = jnp.sum(wide_ref[...], axis=1, keepdims=True) * (1.0 / width)
        same = iota((tok, tok), 1) == iota((tok, tok), 0)
        line = jnp.sum(jnp.where(same, lax.rsqrt(mean + 1e-06), 0.0), axis=0, keepdims=True)
        stat[t] = jnp.broadcast_to(line, (8, tok))
        inv_hop(t).start()

        @pl.loop(2 - t, steps)
        def _(j):
            hop(t, j).start()

        if t == 0:

            @pl.when(edge)
            def _():
                inv_here().start()

                @pl.loop(0, steps)
                def _(j):
                    enter_here(j).start()

    def wd_other(k):
        return (z, 1 - c) if k == 0 else (1 - z, c if k == 1 else 1 - c)

    pair = 2 * OUT_COLS
    pairs = out_steps // 2

    def wd_copy(k, m):
        zz, cc = wd_other(k)
        return remote(
            w_down.at[:, cols_of(m, pair, cc * half)],
            wd.at[part, m],
            wd_send.at[k],
            wd_recv.at[k, m],
            at(y, zz, cc),
        )

    def wd_copy_last(k, i):
        zz, cc = wd_other(k)
        return remote(
            w_down.at[:, cols_of(out_steps - 2 + i, OUT_COLS, cc * half)],
            wd.at[part, pairs - 1, :, i * OUT_COLS : (i + 1) * OUT_COLS],
            wd_send.at[k],
            wd_recv.at[k, pairs - 1 + i],
            at(y, zz, cc),
        )

    def wd_wait(k, n):
        zz, cc = wd_other(k)

        @pl.when((n % 2 == 0) & (n < out_steps - 2))
        def _():
            copy_wait(wd.at[zz * 2 + cc, n // 2], wd_recv.at[k, n // 2])

        for i in range(2):

            @pl.when(n == out_steps - 2 + i)
            def _():
                block = wd.at[zz * 2 + cc, pairs - 1, :, i * OUT_COLS : (i + 1) * OUT_COLS]
                copy_wait(block, wd_recv.at[k, pairs - 1 + i])

    for k in (1, 0):
        wd_copy(k, 0).start()
    copy_wait(stage.at[0], stage_sem.at[0])
    hop(0, 0).start()
    hop(0, 1).start()
    @pl.when(odd == 0)
    def _():
        staging(1, state_a)

    @pl.when(odd == 1)
    def _():
        staging(1, state_b)

    for copy in small:
        copy.wait()
    tri = (iota((tok, tok), 0) < iota((tok, tok), 1)).astype(BF16)
    slot_rows = []
    for t in range(2):
        route = jnp.where(odd == t, route_a[...], route_b[...]).astype(F32)
        onehot = (iota((16, tok), 0).astype(F32) == route).astype(F32)
        earlier = jnp.dot(onehot.astype(BF16), tri, preferred_element_type=F32)
        rank = jnp.sum(onehot * earlier, axis=0, keepdims=True)
        slot_rows.append(route * cap + rank)
    tgt_own[...] = jnp.concatenate(slot_rows + [jnp.zeros((6, tok), F32)], axis=0)
    tgt_copy = remote(tgt_own, tgt_far, tgt_sems.at[0], tgt_sems.at[1], (p, far))
    tgt_copy.start()
    depart(0)
    copy_wait(stage.at[1], stage_sem.at[1])
    hop(1, 0).start()
    depart(1)

    load_gate = pltpu.make_async_copy(w_gate, wgu.at[pl.ds(0, share)], local_sem.at[0])
    load_up = pltpu.make_async_copy(w_up, wgu.at[pl.ds(share, share)], local_sem.at[1])
    load_gate.start()
    load_up.start()

    @pl.loop(0, out_steps // 2)
    def _(m):
        pltpu.make_async_copy(
            w_down.at[:, cols_of(m, 2 * OUT_COLS, c * half)], wd.at[part, m], local_sem.at[2]
        ).start()

    tgt_copy.wait()
    slots = 4 * cap
    r = iota((2 * slots, tok), 0)
    expert = sum((r >= cap2 * k).astype(jnp.int32) for k in range(1, 4))
    rem = r - expert * cap2
    rel = (rem >= cap).astype(jnp.int32)
    value = (expert * cap + rem - rel * cap).astype(F32)

    def column(line):
        same = iota((tok, tok), 1) == iota((tok, tok), 0)
        lines = jnp.broadcast_to(line, (tok, tok))
        return jnp.sum(jnp.where(same, lines, 0.0), axis=1, keepdims=True)

    for t in range(2):
        here = jnp.where((value == tgt_own[t : t + 1, :]) & (rel == 0), 1.0, 0.0)
        there = jnp.where((value == tgt_far[t : t + 1, :]) & (rel == 1), 1.0, 0.0)
        sel_ref[t] = jnp.concatenate([here, there], axis=1).astype(BF16)
        target = column(tgt_own[t : t + 1, :])
        picks = iota((tok, slots), 1).astype(F32) == target
        pick_ref[t] = jnp.where(picks, 1.0, 0.0).astype(BF16)
        weight = jnp.where(odd == t, weight_a[...], weight_b[...])
        weight_ref[t] = jnp.broadcast_to(column(weight), (tok, 128))

    def disp(t, d, j):
        e = turn(d)
        return remote(
            sendbuf.at[j, e],
            rows_ref.at[t, j, c * 4 + y],
            disp_send.at[d - 1, j],
            disp_recv.at[t, d - 1, j],
            at(e, z, c),
        )

    def disp_left(j):
        for d in (1, 2, 3):
            copy_wait(sendbuf.at[j, turn(d)], disp_send.at[d - 1, j])

    def disp_here(t, j):
        return pltpu.make_async_copy(
            sendbuf.at[j, y], rows_ref.at[t, j, c * 4 + y], disp_local.at[t, j]
        )

    def arrive(t, j):
        passed_on = (t == 1) | (inner == 1)
        copy_wait(xbuf.at[t, 1, j], arr_sem.at[t, j])

        @pl.when(passed_on)
        def _():
            across(t, j).start()

        @pl.when(j == 0)
        def _():
            copy_wait(inv_ref.at[t, 1], inv_sems.at[t, 1])

            @pl.when(passed_on)
            def _():
                inv_across(t).start()

    def dispatch(t, j):
        @pl.when(j == 0)
        def _():
            copy_wait(inv_ref.at[t, 0], inv_sems.at[t, 3])
            for side in range(2):
                inv_col[pl.ds(side * tok, tok), :] = jnp.broadcast_to(
                    column(inv_ref[t, side, 0:1, :]), (tok, 128)
                )

        copy_wait(xbuf.at[t, 0, j], home_sem.at[t, j])

        @pl.when(t == 1)
        def _():
            disp_left(j)

        x = xbuf[t, :, j].reshape(2 * tok, STEP).astype(F32)
        normed = (x * inv_col[:, 0:1] * gain_ref[:, cols_of(j, STEP)]).astype(BF16)
        picked = jnp.dot(sel_ref[t], normed, preferred_element_type=F32)
        sendbuf[j] = picked.astype(BF16).reshape(4, cap2, STEP)
        for d in (1, 3, 2):
            disp(t, d, j).start()
        disp_here(t, j).start()

    def cores(t, j):
        block = rows_ref.at[t, j, pl.ds(c * 4, 4)]
        return remote(block, block, core_send.at[t], core_recv.at[t, j], at(y, z, 1 - c))

    def share_rows(t, j):
        for d in (1, 3, 2):
            copy_wait(rows_ref.at[t, j, c * 4 + turn(4 - d)], disp_recv.at[t, d - 1, j])
        disp_here(t, j).wait()
        cores(t, j).start()

    def project(t, j):
        cols = cols_of(j, STEP)
        copy_wait(rows_ref.at[t, j, pl.ds((1 - c) * 4, 4)], core_recv.at[t, j])

        @pl.when(j == 0)
        def _():
            acc[...] = jnp.zeros_like(acc)

        lhs = rows_ref[t, j].reshape(8 * cap2, STEP)
        acc[...] += lax.dot_general(
            lhs, wgu[:, cols], (((1,), (1,)), ((), ())), preferred_element_type=F32
        )

        @pl.when(j == steps - 1)
        def _():
            hidden(t)

    def hid_copy(t, k):
        if k == 0:
            return remote(
                hs.at[t, 0], hid.at[t, part], hid_send.at[t, 0], hid_recv.at[t, 0], at(y, z, 1 - c)
            )
        if k == 1:
            return remote(
                hs.at[t, 1], hid.at[t, part], hid_send.at[t, 1], hid_recv.at[t, 1], (p, far)
            )
        block = hid.at[t, (1 - z) * 2 + c]
        return remote(block, block, hid_send.at[t, 2], hid_recv.at[t, 2], at(y, z, 1 - c))

    def hid_wait(t, k):
        zz, cc = ((z, 1 - c), (1 - z, c), (1 - z, 1 - c))[k]
        copy_wait(hid.at[t, zz * 2 + cc], hid_recv.at[t, k])

    def hidden(t):
        gate, up = acc[:, :share], acc[:, share:]
        h = gate / (1.0 + jnp.exp(-gate)) * up
        mine = [h[b * cap2 : b * cap2 + cap] for b in range(8)]
        others = [h[b * cap2 + cap : (b + 1) * cap2] for b in range(8)]
        hs[t, 1] = jnp.concatenate(others, axis=0).astype(BF16)
        hid_copy(t, 1).start()
        hs[t, 0] = jnp.concatenate(mine, axis=0).astype(BF16)
        hid_copy(t, 0).start()
        hid[t, part] = hs[t, 0]

    def send_down(lo, hi):
        @pl.loop(lo, hi)
        def _(m):
            for k in (1, 2, 0):
                wd_copy(k, m).start()

    def send_down_rest():
        send_down(EARLY // 2, pairs - 1)
        for i in range(2):
            for k in (1, 2, 0):
                wd_copy_last(k, i).start()

    def back(t, k, n):
        d, cc = k // 2, k % 2
        to = (c + cc) % 2
        src = outbuf.at[t, n, to * 4 + turn(d)]
        dst = returned.at[t, n, c, y]
        if k == 0:
            return pltpu.make_async_copy(src, dst, ret_recv.at[t, c, n])
        return remote(src, dst, ret_send.at[t, k], ret_recv.at[t, c, n], at(turn(d), z, to))

    def down_wait(n):
        for k in range(3):
            wd_wait(k, n)

    def down(t, n):
        cols = cols_of(n % 2, OUT_COLS)
        out = jnp.zeros((8 * cap, OUT_COLS), F32)
        for g in range(EGROUP):
            out += jnp.dot(hid[t, g], wd[g, n // 2, :, cols], preferred_element_type=F32)
        outbuf[t, n] = out.reshape(8, cap, OUT_COLS).astype(BF16)
        for k in (4, 5, 2, 3, 6, 7, 1, 0):
            back(t, k, n).start()

    def pass_hidden(t):
        hid_wait(t, 1)
        hid_copy(t, 2).start()

    def have_hidden(t):
        hid_wait(t, 0)
        hid_wait(t, 2)

    def place(side, n):
        at_step = n // (STEP // OUT_COLS)
        return side * (half // STEP) + at_step, cols_of(n % (STEP // OUT_COLS), OUT_COLS)

    def put(t, side, n):
        j, cols = place(side, n)
        return pltpu.make_async_copy(
            xbuf.at[t, 0, j, :, cols],
            news.at[(t + odd) % 2, :, cols_of(n, OUT_COLS, side * half)],
            out_sem.at[t],
        )

    def finish(n):
        for side in range(2):
            j, cols = place(side, n)
            for t in range(2):
                copy_wait(returned.at[t, n, side], ret_recv.at[t, side, n])
                block = returned[t, n, side].astype(F32).reshape(slots, OUT_COLS)
                taken = jnp.dot(pick_ref[t], block.astype(BF16), preferred_element_type=F32)
                home = xbuf[t, 0, j, :, cols].astype(F32)
                xbuf[t, 0, j, :, cols] = (home + taken * weight_ref[t][:, 0:1]).astype(BF16)
                put(t, side, n).start()

    load_gate.wait()
    load_up.wait()
    copy_wait(wd.at[part], local_sem.at[2])

    @pl.loop(0, total + LAG + 1)
    def _(k):
        @pl.when(k < total)
        def _():
            arrive(k // steps, k % steps)

        @pl.when((k >= NEXT) & (k < total + NEXT))
        def _():
            dispatch((k - NEXT) // steps, (k - NEXT) % steps)

        @pl.when((k >= LAG) & (k < total + LAG))
        def _():
            share_rows((k - LAG) // steps, (k - LAG) % steps)

        @pl.when(k >= LAG + 1)
        def _():
            project((k - LAG - 1) // steps, (k - LAG - 1) % steps)

        @pl.when(k == 2)
        def _():
            wd_copy(2, 0).start()

        for n, when in enumerate(FILL, 1):

            @pl.when(k == when)
            def _():
                send_down(n, n + 1)

        @pl.when(k == steps + LAG)
        def _():
            send_down(1 + len(FILL), EARLY // 2)

        @pl.when(k == total + LAG - AHEAD - 2)
        def _():
            pass_hidden(0)

        @pl.when(k == total + LAG - AHEAD)
        def _():
            have_hidden(0)

        @pl.when((k >= total + LAG - AHEAD) & (k < total + LAG))
        def _():
            down_wait(k - (total + LAG - AHEAD))
            down(0, k - (total + LAG - AHEAD))

    send_down_rest()

    @pl.loop(AHEAD, EARLY - 1)
    def _(n):
        down_wait(n)
        down(0, n)

    pass_hidden(1)
    down_wait(EARLY - 1)
    down(0, EARLY - 1)
    have_hidden(1)

    @pl.loop(0, EARLY)
    def _(n):
        down(1, n)

    @pl.loop(EARLY, out_steps)
    def _(n):
        finish(2 * (n - EARLY))
        finish(2 * (n - EARLY) + 1)
        down_wait(n)
        for t in range(2):
            down(t, n)

    pl.loop(2 * (out_steps - EARLY), out_steps)(finish)

    for t in range(2):
        copy_wait(stage.at[t], hi_send.at[t])
        copy_wait(stat.at[t], inv_sems.at[t, 0])

        @pl.when((t == 1) | (inner == 1))
        def _():
            copy_wait(xbuf.at[t, 1], lo_send.at[t])
            copy_wait(inv_ref.at[t, 1], inv_sems.at[t, 2])

        copy_wait(xbuf.at[t, 0], out_sem.at[t])
        copy_wait(rows_ref.at[t, :, pl.ds(c * 4, 4)], core_send.at[t])
        for k in range(3):
            copy_wait(hs.at[t, 0], hid_send.at[t, k])
    for k in range(3):
        copy_wait(wd.at[part], wd_send.at[k])
    pl.loop(0, steps)(disp_left)
    for t in range(2):
        for k in range(1, 8):
            d, cc = k // 2, k % 2
            copy_wait(outbuf.at[t, :, ((c + cc) % 2) * 4 + turn(d)], ret_send.at[t, k])


def local(
    state_a,
    state_b,
    enter_a,
    enter_b,
    route_a,
    route_b,
    weight_a,
    weight_b,
    norm_gain,
    w_gate,
    w_up,
    w_down,
):
    tok, width = enter_a.shape
    sections = lax.axis_size("pp")
    experts = lax.axis_size("ep") // EGROUP
    cap = tok * 5 // (4 * experts)
    cap2 = 2 * cap
    half = width // 2
    share = w_gate.shape[1]
    steps = width // STEP
    out_steps = half // OUT_COLS
    lines = [v.reshape(1, tok) for v in (route_a, route_b, weight_a, weight_b)]
    hbm = pl.BlockSpec(memory_space=pl.ANY)
    dma = pltpu.SemaphoreType.DMA
    news = pl.pallas_call(
        functools.partial(relay_kernel, sections),
        out_shape=jax.ShapeDtypeStruct((2, tok, width), BF16),
        in_specs=[hbm] * 12,
        out_specs=hbm,
        scratch_shapes=[
            pltpu.VMEM((1, tok), jnp.int32),
            pltpu.VMEM((1, tok), jnp.int32),
            pltpu.VMEM((1, tok), F32),
            pltpu.VMEM((1, tok), F32),
            pltpu.VMEM((1, width), F32),
            pltpu.VMEM((2, steps, tok, STEP), BF16),
            pltpu.VMEM((2, 8, tok), F32),
            pltpu.VMEM((tok, 128), F32),
            pltpu.VMEM((2 * tok, 128), F32),
            pltpu.VMEM((2, 2, steps, tok, STEP), BF16),
            pltpu.VMEM((2, 2, 8, tok), F32),
            pltpu.VMEM((8, tok), F32),
            pltpu.VMEM((8, tok), F32),
            pltpu.VMEM((2, experts * cap2, 2 * tok), BF16),
            pltpu.VMEM((2, tok, experts * cap), BF16),
            pltpu.VMEM((2, tok, 128), F32),
            pltpu.VMEM((steps, experts, cap2, STEP), BF16),
            pltpu.VMEM((2, out_steps, 8, cap, OUT_COLS), BF16),
            pltpu.VMEM((2, out_steps, 2, experts, cap, OUT_COLS), BF16),
            pltpu.VMEM((2, steps, 8, cap2, STEP), BF16),
            pltpu.VMEM((2 * share, width), BF16),
            pltpu.VMEM((EGROUP, out_steps // 2, share, 2 * OUT_COLS), BF16),
            pltpu.VMEM((8 * cap2, 2 * share), F32),
            pltpu.VMEM((2, 2, 8 * cap, share), BF16),
            pltpu.VMEM((2, EGROUP, 8 * cap, share), BF16),
            dma((8,)),
            dma((2,)),
            dma((2,)),
            dma((2, 4)),
            dma((2,)),
            dma((2, steps)),
            dma((2, steps)),
            dma((2,)),
            dma((2,)),
            dma((3, steps)),
            dma((2, 3, steps)),
            dma((2, steps)),
            dma((2,)),
            dma((2, steps)),
            dma((2, 3)),
            dma((2, 3)),
            dma((3,)),
            dma((3, out_steps // 2 + 1)),
            dma((2, 8)),
            dma((2, 2, out_steps)),
        ],
        compiler_params=pltpu.CompilerParams(
            collective_id=0, has_side_effects=True, vmem_limit_bytes=62 * 2**20
        ),
        name="relay",
    )(
        *lines,
        norm_gain,
        state_a[0],
        state_b[0],
        enter_a,
        enter_b,
        w_gate[0],
        w_up[0],
        w_down[0],
    )
    return (news[0:1], news[1:2])


def solution(mesh):
    return jax.shard_map(
        local,
        mesh=mesh,
        in_specs=(
            P("pp", "ep", None),
            P("pp", "ep", None),
            P("ep", None),
            P("ep", None),
            P("pp", "ep", None),
            P("pp", "ep", None),
            P("pp", "ep", None),
            P("pp", "ep", None),
            P("pp", None),
            P("pp", "ep", None),
            P("pp", "ep", None),
            P("pp", "ep", None),
        ),
        out_specs=(P("pp", "ep", None), P("pp", "ep", None)),
        check_vma=False,
    )
```
